128 devices in a mesh: dp: 4 (over x_lo, core), row: 16 (over z, y), col: 2 (over x_hi).
Axes of the slice: x: 4 (x_hi: 2, x_lo: 2; x = x_hi * 2 + x_lo), y: 4, z: 4, core: 2. Of those that a mesh axis runs over, the one named last changes fastest.
Arguments:
- features: bfloat16 [4096, 4096], P('dp', 'row')
- codes: int32 [4096, 512], P('dp', 'col'), may hold values from 0 to 255
- codebooks: bfloat16 [512, 256, 8], P('col')
Outputs:
- rotation: float32 [4096, 4096], P(('row', 'dp'), 'col')
The draws below stay inside these ranges and needn't reach their ends.
All inputs are finite; a program needn't handle non-finite values.
Results may differ from the reference program's by a relative error of at most 0.00075.
Values sent between devices are 32-bit elements; how exact they have to be, the bound alone decides.
No kernel may reach another device: no remote copies, remote signals or barrier semaphores. Data moves between devices by JAX's collectives and lax.ppermute only.
A program may use at most 64 MiB of HBM per device.

```python
import math
import jax
import jax.numpy as jnp
from jax import lax

D = 4096
M = 512
CODES = 256
SUBDIM = 8
ITERS = 2
SAMPLES = 4096


def shared_codes(key):
    return jax.random.randint(jax.random.fold_in(key, 101), (SAMPLES, M), 0, CODES, dtype=jnp.int32)


def shared_codebooks(key):
    values = jax.random.normal(jax.random.fold_in(key, 202), (M, CODES, SUBDIM), jnp.float32)
    return jnp.clip(values, -6.0, 6.0).astype(jnp.bfloat16)


def draw_codes(key, part):
    return shared_codes(key)


def draw_codebooks(key, part):
    return shared_codebooks(key)


def draw_features(key, part):
    codes = shared_codes(key)
    codebooks = shared_codebooks(key).astype(jnp.float32)
    key = jax.random.fold_in(key, 11)
    first, second, third = jax.random.split(key, 3)
    subspace = jnp.arange(M, dtype=jnp.int32)[None, :]
    rebuilt = codebooks[subspace, codes].reshape(SAMPLES, D)
    position = jnp.arange(D, dtype=jnp.float32) / D
    mixing = jax.random.uniform(third, (D,), jnp.float32, -0.7, 0.7)
    own_scale = jnp.exp(jax.random.uniform(second, (D,), jnp.float32, 0.0, math.log(2.0)))
    own_scale = own_scale * jnp.exp(math.log(2.0) * position)
    noise = 0.5 * jax.random.normal(first, (SAMPLES, D), jnp.float32)
    partner = jnp.roll(rebuilt, D // 2 + 3, axis=1)
    values = own_scale[None, :] * (rebuilt + mixing[None, :] * partner) + noise
    return values.astype(jnp.bfloat16)


def setup_inputs(seed: int = 0) -> dict:
    seeds = jax.random.split(jax.random.key(seed), 4)
    return {
        "features": draw_features(jax.random.fold_in(seeds[3], 71), 0),
        "codes": draw_codes(jax.random.fold_in(seeds[3], 71), 0),
        "codebooks": draw_codebooks(jax.random.fold_in(seeds[3], 71), 0),
    }


epsilon = 1e-06
start_scale = 0.45

def decode(codes, codebooks):
    subspace = jnp.arange(codebooks.shape[0], dtype=jnp.int32)[None, :]
    picked = codebooks[subspace, codes]
    return picked.reshape(codes.shape[0], -1)

def reference(features, codes, codebooks):
    rebuilt = decode(codes, codebooks).astype(jnp.float32)
    covariance = jnp.dot(features.astype(jnp.float32).T, rebuilt, precision=lax.Precision.HIGHEST)
    sum_squares = jnp.sum(covariance * covariance)
    rotation = covariance * (start_scale * jnp.sqrt(D / (sum_squares + epsilon)))
    for sweep in range(ITERS):
        gram_matrix = jnp.dot(rotation.T, rotation, precision=lax.Precision.HIGHEST)
        rotation = 1.5 * rotation - 0.5 * jnp.dot(rotation, gram_matrix, precision=lax.Precision.HIGHEST)
    return rotation
```

```python
import functools

import jax
import jax.numpy as jnp
from jax import lax
from jax.experimental import pallas as pl
from jax.experimental.pallas import tpu as pltpu
from jax.sharding import Mesh, PartitionSpec as P

ITERS = 2

epsilon = 1e-06
start_scale = 0.45

F32 = jnp.float32
BF16 = jnp.bfloat16
AXES = ("xl", "core", "z", "y", "xh")
VMEM_BYTES = 48 * 1024 * 1024

NN = (((1,), (0,)), ((), ()))
NT = (((1,), (1,)), ((), ()))


def split(value):
    high = value.astype(BF16)
    return high, (value - high.astype(F32)).astype(BF16)


def dot3(a, b, dims):
    dot = functools.partial(lax.dot_general, dimension_numbers=dims, preferred_element_type=F32)
    return dot(a[0], b[0]) + (dot(a[0], b[1]) + dot(a[1], b[0]))


def call(kernel, out_shape, operands, scratch=(), flops=0, n_scalars=1):
    vmem = pl.BlockSpec(memory_space=pltpu.VMEM)
    smem = pl.BlockSpec(memory_space=pltpu.SMEM)
    moved = sum(o.size * o.dtype.itemsize for o in operands)
    moved += sum(o.size * o.dtype.itemsize for o in out_shape)
    return pl.pallas_call(
        kernel,
        out_shape=out_shape,
        in_specs=[smem] * n_scalars + [vmem] * (len(operands) - n_scalars),
        out_specs=[vmem] * len(out_shape),
        scratch_shapes=scratch,
        compiler_params=pltpu.CompilerParams(vmem_limit_bytes=VMEM_BYTES),
        cost_estimate=pl.CostEstimate(flops=flops, bytes_accessed=moved, transcendentals=0),
    )(*operands)


def covariance_kernel(where, features, codes, table, give, keep, turned, index, rebuilt):
    core = where[0]
    samples = codes.shape[0]
    turned[...] = features[...].astype(F32).T.astype(BF16)
    index[...] = codes[...].T
    groups = rebuilt.shape[0] // 16
    for place, out in enumerate((give, keep)):
        target = lax.rem(core + 1 + place, 2)
        for part in range(out.shape[1] // rebuilt.shape[0]):
            start = target * (out.shape[1] // 8) + part * (rebuilt.shape[0] // 8)

            def pair(step, carry):
                first = start + 2 * step
                rows = pl.ds(pl.multiple_of(first * 8, 16), 16)
                words = table[rows, :].astype(F32)
                decoded = []
                for which in range(2):
                    low = words[8 * which : 8 * which + 8, :128]
                    high = words[8 * which : 8 * which + 8, 128:]
                    code = index[pl.ds(first + which, 1), :]
                    pieces = []
                    for block in range(samples // 128):
                        picked = jnp.broadcast_to(code[:, block * 128 : block * 128 + 128], (8, 128))
                        place_in = picked & 127
                        a = jnp.take_along_axis(low, place_in, axis=1, mode="promise_in_bounds")
                        b = jnp.take_along_axis(high, place_in, axis=1, mode="promise_in_bounds")
                        pieces.append(jnp.where(picked < 128, a, b))
                    decoded.append(jnp.concatenate(pieces, axis=1))
                rebuilt[pl.ds(pl.multiple_of(step * 16, 16), 16), :] = jnp.concatenate(
                    decoded, axis=0
                ).astype(BF16)
                return carry

            lax.fori_loop(0, groups, pair, 0)
            width = rebuilt.shape[0]
            out[:, part * width : part * width + width] = lax.dot_general(
                turned[...], rebuilt[...], NT, preferred_element_type=F32
            )


def covariance_part(where, features, codes, table):
    samples, rows = features.shape
    quarter = codes.shape[1] * 4
    out = jax.ShapeDtypeStruct((rows, quarter), F32)
    return call(
        covariance_kernel,
        [out, out],
        [where, features, codes, table],
        [
            pltpu.VMEM((rows, samples), BF16),
            pltpu.VMEM((codes.shape[1], samples), jnp.int32),
            pltpu.VMEM((256, samples), BF16),
        ],
        flops=2 * samples * rows * quarter * 2 + 16000000000,
    )


def gram_kernel(place, where, *refs):
    left_refs, right_refs = refs[:4], (refs[0],) + refs[4:7]
    out, left_high, left_low, right_high, right_low = refs[7:]
    core, x = where[0], where[1]
    half = out.shape[1]
    row = pl.multiple_of(lax.rem(core + place, 2) * half, half)
    for block in range(4):
        rows = slice(block * half, block * half + half)
        left_high[rows, :], left_low[rows, :] = split(left_refs[block][pl.ds(row, half), :])
        rows = slice(block * 2 * half, block * 2 * half + 2 * half)
        right_high[rows, :], right_low[rows, :] = split(right_refs[block][...])
    for step in range(4):
        quarter = pl.ds(pl.multiple_of(lax.rem(x + step, 4) * half, half), half)
        out[step] = dot3(
            (left_high[quarter, :], left_low[quarter, :]), (right_high[...], right_low[...]), NT
        )


def gram_part(place, where, own, near_y, near_z):
    rows, depth = own.shape
    half = rows // 2
    return call(
        functools.partial(gram_kernel, place),
        [jax.ShapeDtypeStruct((4, half, 4 * rows), F32)],
        [where, own, *near_y, *near_z],
        [
            pltpu.VMEM((4 * half, depth), BF16),
            pltpu.VMEM((4 * half, depth), BF16),
            pltpu.VMEM((4 * rows, depth), BF16),
            pltpu.VMEM((4 * rows, depth), BF16),
        ],
        flops=6 * 4 * half * depth * 4 * rows,
    )[0]


def product_kernel(where, scale, *refs):
    ours, theirs = refs[:4], refs[4:8]
    left_refs, right_refs = refs[8:12], (refs[8],) + refs[12:15]
    along_y, along_z = refs[15:19], refs[19:23]
    gram_high, gram_low, right_high, right_low, left_high, left_low = refs[23:]
    core, x = where[0], where[1]
    half = ours[0].shape[0]
    rows, width = along_y[0].shape
    factor = scale[0]
    factor = factor * factor
    for step in range(4):
        quarter = lax.rem(x + step, 4) * 2
        for which, pieces in enumerate((ours, theirs)):
            start = (quarter + lax.rem(core + which, 2)) * half
            place = pl.ds(pl.multiple_of(start, half), half)
            gram_high[place, :], gram_low[place, :] = split(pieces[step][...] * factor)
    for block in range(4):
        place = slice(block * rows, block * rows + rows)
        right_high[place, :], right_low[place, :] = split(right_refs[block][:, :width])
        left_high[:, place], left_low[:, place] = split(left_refs[block][:, width:].T)
    for block in range(4):
        place = slice(block * rows, block * rows + rows)
        along_y[block][...] = dot3(
            (gram_high[place, :], gram_low[place, :]), (right_high[...], right_low[...]), NN
        )
        along_z[block][...] = dot3(
            (left_high[...], left_low[...]), (gram_high[:, place], gram_low[:, place]), NN
        ).T


def product_part(where, scale, ours, theirs, own, near_y, near_z):
    rows, depth = own.shape
    width = depth // 2
    out = jax.ShapeDtypeStruct((rows, width), F32)
    size = 4 * rows
    outs = call(
        product_kernel,
        [out] * 8,
        [where, scale, *ours, *theirs, own, *near_y, *near_z],
        [
            pltpu.VMEM((size, size), BF16),
            pltpu.VMEM((size, size), BF16),
            pltpu.VMEM((size, width), BF16),
            pltpu.VMEM((size, width), BF16),
            pltpu.VMEM((width, size), BF16),
            pltpu.VMEM((width, size), BF16),
        ],
        flops=6 * size * size * depth,
        n_scalars=2,
    )
    return outs[:4], outs[4:]


def line(axis, shift):
    pairs = [(i, (i + shift) % 4) for i in range(4)]
    if axis == "x":
        spot = [0, 2, 1, 3]
        return ("xl", "xh"), [(spot[a], spot[b]) for a, b in pairs]
    return axis, pairs


def send(value, axis, shift):
    return lax.ppermute(value, *line(axis, shift))


def swap(value, axis):
    return lax.ppermute(value, axis, [(0, 1), (1, 0)])


def total(value):
    value = jnp.broadcast_to(value, (8, 128))
    value = value + swap(value, "core")
    for axis in ("xl", "xh"):
        value = value + swap(value, axis)
    for axis in ("z", "y"):
        value = value + lax.ppermute(value, axis, [(i, i ^ 1) for i in range(4)])
        value = value + lax.ppermute(value, axis, [(i, i ^ 2) for i in range(4)])
    return value[0, 0]


def on_device(features, codes, codebooks):
    core = lax.axis_index("core")
    xl = lax.axis_index("xl")
    x = lax.axis_index("xh") * 2 + xl
    where = jnp.stack([core, x]).astype(jnp.int32)

    table = jnp.swapaxes(codebooks, 1, 2).reshape(-1, codebooks.shape[1])
    table_half = table.shape[0] // 2
    codes_half = codes.shape[1] // 2

    def half(which):
        return covariance_part(
            where,
            features,
            lax.dynamic_slice_in_dim(codes, which * codes_half, codes_half, 1),
            lax.dynamic_slice_in_dim(table, which * table_half, table_half, 0),
        )

    give, keep = half(1 - xl)
    theirs = swap(keep + swap(give, "core"), "xl")
    give, keep = half(xl)
    current = (keep + swap(give, "core")) + theirs
    dimensions = features.shape[1] * 16
    sum_squares = total(jnp.sum(current * current))
    scale = start_scale * jnp.sqrt(dimensions / (sum_squares + epsilon))

    for sweep in range(ITERS):
        near_y = [send(current, "y", -d) for d in (1, 2, 3)]
        near_z = [send(current, "z", -d) for d in (1, 2, 3)]
        give = gram_part(1, where, current, near_y, near_z)
        from_core = swap(give, "core")
        keep = gram_part(0, where, current, near_y, near_z)
        part = keep + from_core
        mine = part[0]
        for d in (1, 2, 3):
            mine = mine + send(part[d], "x", d)
        ours = [mine] + [send(mine, "x", -d) for d in (1, 2, 3)]
        other = [swap(piece, "core") for piece in ours]
        factor = scale if sweep == 0 else jnp.float32(1)
        along_y, along_z = product_part(
            where, factor[None], ours, other, current, near_y, near_z
        )
        sums = []
        for axis, pieces in (("y", along_y), ("z", along_z)):
            value = pieces[0]
            for d in (1, 2, 3):
                value = value + send(pieces[d], axis, d)
            sums.append(value)
        current = factor * (1.5 * current - 0.5 * jnp.concatenate(sums, axis=1))

    rank = xl * 2 + core
    rows = current.shape[0] // 4
    width = current.shape[1]
    out = jnp.zeros((rows, 4 * width), F32)
    for d in range(4):
        piece = lax.dynamic_slice_in_dim(current, (rank ^ d) * rows, rows, 0)
        if d:
            piece = lax.ppermute(piece, ("xl", "core"), [(i, i ^ d) for i in range(4)])
        out = lax.dynamic_update_slice_in_dim(out, piece, (rank ^ d) * width, 1)
    return out


def solution(mesh):
    devices = mesh.devices.reshape(2, 2, 4, 4, 2)
    return jax.shard_map(
        on_device,
        mesh=Mesh(devices, AXES),
        in_specs=(
            P(("xl", "core"), ("z", "y")),
            P(("xl", "core"), "xh"),
            P("xh", None, None),
        ),
        out_specs=P(("z", "y", "xl", "core"), "xh"),
        check_vma=False,
    )
```

```python
import functools

import jax
import jax.numpy as jnp
from jax import lax
from jax.experimental import pallas as pl
from jax.experimental.pallas import tpu as pltpu
from jax.sharding import Mesh, PartitionSpec as P

ITERS = 2

epsilon = 1e-06
start_scale = 0.45

F32 = jnp.float32
BF16 = jnp.bfloat16
AXES = ("xl", "core", "z", "y", "xh")
VMEM_BYTES = 48 * 1024 * 1024

NN = (((1,), (0,)), ((), ()))
NT = (((1,), (1,)), ((), ()))


def split(value):
    high = value.astype(BF16)
    return high, (value - high.astype(F32)).astype(BF16)


def dot3(a, b, dims):
    dot = functools.partial(lax.dot_general, dimension_numbers=dims, preferred_element_type=F32)
    return dot(a[0], b[0]) + (dot(a[0], b[1]) + dot(a[1], b[0]))


def call(kernel, out_shape, operands, scratch=(), flops=0, n_scalars=1):
    vmem = pl.BlockSpec(memory_space=pltpu.VMEM)
    smem = pl.BlockSpec(memory_space=pltpu.SMEM)
    moved = sum(o.size * o.dtype.itemsize for o in operands)
    moved += sum(o.size * o.dtype.itemsize for o in out_shape)
    return pl.pallas_call(
        kernel,
        out_shape=out_shape,
        in_specs=[smem] * n_scalars + [vmem] * (len(operands) - n_scalars),
        out_specs=[vmem] * len(out_shape),
        scratch_shapes=scratch,
        compiler_params=pltpu.CompilerParams(vmem_limit_bytes=VMEM_BYTES),
        cost_estimate=pl.CostEstimate(flops=flops, bytes_accessed=moved, transcendentals=0),
    )(*operands)


def covariance_kernel(where, features, codes, table, give, keep, turned, index, rebuilt):
    core = where[0]
    samples = codes.shape[0]
    turned[...] = features[...].astype(F32).T.astype(BF16)
    index[...] = codes[...].T
    groups = rebuilt.shape[0] // 16
    for place, out in enumerate((give, keep)):
        target = lax.rem(core + 1 + place, 2)
        for part in range(out.shape[1] // rebuilt.shape[0]):
            start = target * (out.shape[1] // 8) + part * (rebuilt.shape[0] // 8)

            def pair(step, carry):
                first = start + 2 * step
                rows = pl.ds(pl.multiple_of(first * 8, 16), 16)
                words = table[rows, :].astype(F32)
                decoded = []
                for which in range(2):
                    low = words[8 * which : 8 * which + 8, :128]
                    high = words[8 * which : 8 * which + 8, 128:]
                    code = index[pl.ds(first + which, 1), :]
                    pieces = []
                    for block in range(samples // 128):
                        picked = jnp.broadcast_to(code[:, block * 128 : block * 128 + 128], (8, 128))
                        place_in = picked & 127
                        a = jnp.take_along_axis(low, place_in, axis=1, mode="promise_in_bounds")
                        b = jnp.take_along_axis(high, place_in, axis=1, mode="promise_in_bounds")
                        pieces.append(jnp.where(picked < 128, a, b))
                    decoded.append(jnp.concatenate(pieces, axis=1))
                rebuilt[pl.ds(pl.multiple_of(step * 16, 16), 16), :] = jnp.concatenate(
                    decoded, axis=0
                ).astype(BF16)
                return carry

            lax.fori_loop(0, groups, pair, 0, unroll=True)
            width = rebuilt.shape[0]
            out[:, part * width : part * width + width] = lax.dot_general(
                turned[...], rebuilt[...], NT, preferred_element_type=F32
            )


def covariance_part(where, features, codes, table):
    samples, rows = features.shape
    quarter = codes.shape[1] * 4
    out = jax.ShapeDtypeStruct((rows, quarter), F32)
    return call(
        covariance_kernel,
        [out, out],
        [where, features, codes, table],
        [
            pltpu.VMEM((rows, samples), BF16),
            pltpu.VMEM((codes.shape[1], samples), jnp.int32),
            pltpu.VMEM((256, samples), BF16),
        ],
    )


KEPT = (3, 4, 3)


def offsets(rows):
    starts = [0]
    for count in KEPT:
        starts.append(starts[-1] + count * rows)
    return starts


def share(where, step, which):
    return lax.rem(where[1] + step, 4) * 2 + lax.rem(where[0] + which, 2)


def gram_kernel(where, own, y1, y2, z1, z2, z3, give, keep, squares, rh, rl, gram):
    rows = own.shape[0]
    column = jnp.zeros((8, own.shape[1]), F32)
    for block, ref in enumerate((own, z1, z2, z3)):
        place = slice(block * rows, block * rows + rows)
        value = ref[...]
        rh[place, :], rl[place, :] = split(value)
        column = column + jnp.sum((value * value).reshape(rows // 8, 8, -1), axis=0)
    squares[...] = jnp.sum(column.reshape(8, -1, 128), axis=1)
    starts = offsets(rows)
    for block, ref in enumerate((own, y1, y2)):
        width = KEPT[block] * rows
        gram[:, starts[block] : starts[block + 1]] = dot3(
            split(ref[...]), (rh[:width, :], rl[:width, :]), NT
        )
    piece = rows // 8
    for step in range(4):
        for which, out in ((0, keep), (1, give)):
            start = share(where, step, which) * piece
            out[step] = gram[pl.ds(pl.multiple_of(start, 8), piece), :]


def gram_part(where, own, near):
    rows, depth = own.shape
    width = sum(KEPT) * rows
    out = jax.ShapeDtypeStruct((4, rows // 8, width), F32)
    return call(
        gram_kernel,
        [out, out, jax.ShapeDtypeStruct((8, 128), F32)],
        [where, own, *near],
        [pltpu.VMEM((4 * rows, depth), BF16)] * 2 + [pltpu.VMEM((rows, width), F32)],
        flops=6 * rows * width * depth,
    )


def product_kernel(where, scale, *refs):
    shares = refs[0:4], refs[4:8]
    own, y1, y2, z1, z2, z3 = refs[8:14]
    to_own, to_y1, to_y2, to_z1, to_z2, to_z3 = refs[14:20]
    gram, rh, rl, lh, ll = refs[20:]
    rows = own.shape[0]
    factor = scale[0]
    factor = factor * factor
    for step in range(4):
        for which in range(2):
            value = shares[which][step][...] * factor
            start = share(where, step, which) * value.shape[0]
            gram[pl.ds(pl.multiple_of(start, 8), value.shape[0]), :] = value
    for block, ref in enumerate((own, z1, z2, z3)):
        place = slice(block * rows, block * rows + rows)
        rh[place, :], rl[place, :] = split(ref[...])
    for block, ref in enumerate((own, y1, y2)):
        place = slice(block * rows, block * rows + rows)
        lh[place, :], ll[place, :] = split(ref[...])
    starts = offsets(rows)

    def blocks(dy, first, last):
        return gram[:, starts[dy] + first * rows : starts[dy] + last * rows]

    def along(dy, first, last):
        place = slice(first * rows, last * rows)
        return dot3(split(blocks(dy, first, last)), (rh[place, :], rl[place, :]), NN)

    def across(dz, first, last):
        turned = [blocks(dy, dz, dz + 1).T for dy in range(first, last)]
        turned = turned[0] if len(turned) == 1 else jnp.concatenate(turned, axis=1)
        place = slice(first * rows, last * rows)
        return dot3(split(turned), (lh[place, :], ll[place, :]), NN)

    to_y1[...] = along(1, 0, 4)
    to_z1[...] = across(1, 0, 3)
    to_y2[...] = along(2, 1, 3)
    to_z2[...] = across(2, 1, 2)
    to_z3[...] = across(3, 1, 2)
    to_own[...] = along(0, 0, 3) + across(0, 1, 3)


def product_part(where, scale, shares, own, near):
    rows, depth = own.shape
    out = jax.ShapeDtypeStruct((rows, depth), F32)
    return call(
        product_kernel,
        [out] * 6,
        [where, scale, *shares, own, *near],
        [pltpu.VMEM((rows, sum(KEPT) * rows), F32)]
        + [pltpu.VMEM((4 * rows, depth), BF16)] * 2
        + [pltpu.VMEM((3 * rows, depth), BF16)] * 2,
        flops=6 * 16 * rows * rows * depth,
        n_scalars=2,
    )


def line(axis, shift):
    pairs = [(i, (i + shift) % 4) for i in range(4)]
    if axis == "x":
        spot = [0, 2, 1, 3]
        return ("xl", "xh"), [(spot[a], spot[b]) for a, b in pairs]
    return axis, pairs


def send(value, axis, shift):
    return lax.ppermute(value, *line(axis, shift))


def swap(value, axis):
    return lax.ppermute(value, axis, [(0, 1), (1, 0)])


def total_steps():
    return [
        lambda v: v + swap(v, "core"),
        lambda v: v + lax.ppermute(v, "y", [(i, i ^ 1) for i in range(4)]),
        lambda v: v + lax.ppermute(v, "y", [(i, i ^ 2) for i in range(4)]),
        lambda v: v + swap(v, "xl"),
        lambda v: v + swap(v, "xh"),
    ]


def sum_over_x(give, keep):
    other = swap(give, "core")
    mine = keep[0] + other[0]
    for d in (2, 1, 3):
        mine = mine + send(keep[d] + other[d], "x", d)
    return mine


def spread_over_x(mine):
    ours = [mine] + [send(mine, "x", -d) for d in (1, 2, 3)]
    return ours + [swap(piece, "core") for piece in ours]


def on_device(features, codes, codebooks):
    core = lax.axis_index("core")
    xl = lax.axis_index("xl")
    x = lax.axis_index("xh") * 2 + xl
    where = jnp.stack([core, x]).astype(jnp.int32)

    table = jnp.swapaxes(codebooks, 1, 2).reshape(-1, codebooks.shape[1])
    table_half = table.shape[0] // 2
    codes_half = codes.shape[1] // 2

    def half(which, features):
        return covariance_part(
            where,
            features,
            lax.dynamic_slice_in_dim(codes, which * codes_half, codes_half, 1),
            lax.dynamic_slice_in_dim(table, which * table_half, table_half, 0),
        )

    give, keep = half(1 - xl, features)
    theirs, features = lax.optimization_barrier((keep + swap(give, "core"), features))
    theirs = swap(theirs, "xl")
    give, keep = half(xl, features)
    current = (keep + swap(give, "core")) + theirs
    dimensions = features.shape[1] * 16
    moves = (("y", 1), ("z", 1), ("z", -1), ("y", 2), ("z", 2))

    for sweep in range(ITERS):
        y1, z1, z3, y2, z2 = [send(current, axis, -d) for axis, d in moves]
        near = y1, y2, z1, z2, z3
        give, keep, squares = gram_part(where, current, near)
        shares = sum_over_x(give, keep)
        if sweep == 0:
            squares = jnp.broadcast_to(jnp.sum(squares), (8, 128))
            steps = total_steps()
            for step in steps[:3]:
                squares = step(squares)
            shares, squares = lax.optimization_barrier((shares, squares))
            for step in steps[3:]:
                squares = step(squares)
            factor = start_scale * jnp.sqrt(dimensions / (squares[0, 0] + epsilon))
        else:
            factor = jnp.float32(1)
        shares = spread_over_x(shares)
        value, to_y1, to_y2, to_z1, to_z2, to_z3 = product_part(
            where, factor[None], shares, current, near
        )
        for piece, (axis, d) in zip((to_y1, to_z1, to_z3, to_y2, to_z2), moves):
            value = value + send(piece, axis, d)
        current = factor * (1.5 * current - 0.5 * value)

    rank = xl * 2 + core
    rows = current.shape[0] // 4
    width = current.shape[1]
    out = jnp.zeros((rows, 4 * width), F32)
    for d in range(4):
        piece = lax.dynamic_slice_in_dim(current, (rank ^ d) * rows, rows, 0)
        if d:
            piece = lax.ppermute(piece, ("xl", "core"), [(i, i ^ d) for i in range(4)])
        out = lax.dynamic_update_slice_in_dim(out, piece, (rank ^ d) * width, 1)
    return out


def solution(mesh):
    devices = mesh.devices.reshape(2, 2, 4, 4, 2)
    return jax.shard_map(
        on_device,
        mesh=Mesh(devices, AXES),
        in_specs=(
            P(("xl", "core"), ("z", "y")),
            P(("xl", "core"), "xh"),
            P("xh", None, None),
        ),
        out_specs=P(("z", "y", "xl", "core"), "xh"),
        check_vma=False,
    )
```

```python
import functools

import jax
import jax.numpy as jnp
from jax import lax
from jax.experimental import pallas as pl
from jax.experimental.pallas import tpu as pltpu
from jax.sharding import Mesh, PartitionSpec as P

ITERS = 2

epsilon = 1e-06
start_scale = 0.45

F32 = jnp.float32
BF16 = jnp.bfloat16
AXES = ("xl", "core", "z", "y", "xh")
VMEM_BYTES = 48 * 1024 * 1024

NN = (((1,), (0,)), ((), ()))
NT = (((1,), (1,)), ((), ()))


def split(value):
    high = value.astype(BF16)
    return high, (value - high.astype(F32)).astype(BF16)


def dot3(a, b, dims):
    dot = functools.partial(lax.dot_general, dimension_numbers=dims, preferred_element_type=F32)
    return dot(a[0], b[0]) + (dot(a[0], b[1]) + dot(a[1], b[0]))


def call(kernel, out_shape, operands, scratch=(), flops=0, n_scalars=1):
    vmem = pl.BlockSpec(memory_space=pltpu.VMEM)
    smem = pl.BlockSpec(memory_space=pltpu.SMEM)
    moved = sum(o.size * o.dtype.itemsize for o in operands)
    moved += sum(o.size * o.dtype.itemsize for o in out_shape)
    return pl.pallas_call(
        kernel,
        out_shape=out_shape,
        in_specs=[smem] * n_scalars + [vmem] * (len(operands) - n_scalars),
        out_specs=[vmem] * len(out_shape),
        scratch_shapes=scratch,
        compiler_params=pltpu.CompilerParams(vmem_limit_bytes=VMEM_BYTES),
        cost_estimate=pl.CostEstimate(flops=flops, bytes_accessed=moved, transcendentals=0),
    )(*operands)


def covariance_kernel(where, features, codes, table, give, keep, turned, index, rebuilt):
    core, half = where[0], where[2]
    samples, count = codes.shape[0], index.shape[0]
    turned[...] = features[...].astype(F32).T.astype(BF16)
    index[...] = codes[:, pl.ds(pl.multiple_of(half * count, count), count)].T
    groups = rebuilt.shape[0] // 16
    for place, out in enumerate((give, keep)):
        target = lax.rem(core + 1 + place, 2)
        for part in range(out.shape[1] // rebuilt.shape[0]):
            start = target * (out.shape[1] // 8) + part * (rebuilt.shape[0] // 8)

            def pair(step, carry):
                first = start + 2 * step
                rows = pl.ds(pl.multiple_of((half * count + first) * 8, 16), 16)
                words = table[rows, :].astype(F32)
                decoded = []
                for which in range(2):
                    low = words[8 * which : 8 * which + 8, :128]
                    high = words[8 * which : 8 * which + 8, 128:]
                    code = index[pl.ds(first + which, 1), :]
                    pieces = []
                    for block in range(samples // 128):
                        picked = jnp.broadcast_to(code[:, block * 128 : block * 128 + 128], (8, 128))
                        place_in = picked & 127
                        a = jnp.take_along_axis(low, place_in, axis=1, mode="promise_in_bounds")
                        b = jnp.take_along_axis(high, place_in, axis=1, mode="promise_in_bounds")
                        pieces.append(jnp.where(picked < 128, a, b))
                    decoded.append(jnp.concatenate(pieces, axis=1))
                rebuilt[pl.ds(pl.multiple_of(step * 16, 16), 16), :] = jnp.concatenate(
                    decoded, axis=0
                ).astype(BF16)
                return carry

            lax.fori_loop(0, groups, pair, 0, unroll=True)
            width = rebuilt.shape[0]
            out[:, part * width : part * width + width] = lax.dot_general(
                turned[...], rebuilt[...], NT, preferred_element_type=F32
            )


def covariance_part(where, features, codes, table):
    samples, rows = features.shape
    quarter = codes.shape[1] * 2
    out = jax.ShapeDtypeStruct((rows, quarter), F32)
    return call(
        covariance_kernel,
        [out, out],
        [where, features, codes, table],
        [
            pltpu.VMEM((rows, samples), BF16),
            pltpu.VMEM((codes.shape[1] // 2, samples), jnp.int32),
            pltpu.VMEM((256, samples), BF16),
        ],
    )


KEPT = (3, 4, 3)


def offsets(rows):
    starts = [0]
    for count in KEPT:
        starts.append(starts[-1] + count * rows)
    return starts


def share(where, step, which):
    return lax.rem(where[1] + step, 4) * 2 + lax.rem(where[0] + which, 2)


def gram_kernel(where, own, y1, z1, z3, y2, z2, give, keep, rh, rl, gram):
    rows = own.shape[0]
    column = jnp.zeros((8, own.shape[1]), F32)
    for block, ref in enumerate((own, z1, z2, z3)):
        place = slice(block * rows, block * rows + rows)
        value = ref[...]
        rh[place, :], rl[place, :] = split(value)
        column = column + jnp.sum((value * value).reshape(rows // 8, 8, -1), axis=0)
    squares = jnp.sum(column.reshape(8, -1, 128), axis=1)
    starts = offsets(rows)
    for block, ref in enumerate((own, y1, y2)):
        width = KEPT[block] * rows
        gram[:, starts[block] : starts[block + 1]] = dot3(
            split(ref[...]), (rh[:width, :], rl[:width, :]), NT
        )
    piece = rows // 8
    for step in range(4):
        for which, out in ((0, keep), (1, give)):
            start = share(where, step, which) * piece
            out[step, :, : starts[-1]] = gram[pl.ds(pl.multiple_of(start, 8), piece), :]
            out[step, :8, starts[-1] :] = squares
            out[step, 8:, starts[-1] :] = jnp.zeros((piece - 8, 128), F32)


def gram_part(where, own, near):
    rows, depth = own.shape
    width = sum(KEPT) * rows
    out = jax.ShapeDtypeStruct((4, rows // 8, width + 128), F32)
    return call(
        gram_kernel,
        [out, out],
        [where, own, *near],
        [pltpu.VMEM((4 * rows, depth), BF16)] * 2 + [pltpu.VMEM((rows, width), F32)],
        flops=6 * rows * width * depth,
    )


def product_kernel(where, scale, *refs):
    shares = refs[0:4], refs[4:8]
    own, y1, z1, z3, y2, z2 = refs[8:14]
    to_own, to_y1, to_z1, to_z3, to_y2, to_z2 = refs[14:20]
    gram, rh, rl, lh, ll = refs[20:]
    rows = own.shape[0]
    factor = scale[0]
    factor = factor * factor
    for step in range(4):
        for which in range(2):
            value = shares[which][step][:, : gram.shape[1]] * factor
            start = share(where, step, which) * value.shape[0]
            gram[pl.ds(pl.multiple_of(start, 8), value.shape[0]), :] = value
    for block, ref in enumerate((own, z1, z2, z3)):
        place = slice(block * rows, block * rows + rows)
        rh[place, :], rl[place, :] = split(ref[...])
    for block, ref in enumerate((own, y1, y2)):
        place = slice(block * rows, block * rows + rows)
        lh[place, :], ll[place, :] = split(ref[...])
    starts = offsets(rows)

    def blocks(dy, first, last):
        return gram[:, starts[dy] + first * rows : starts[dy] + last * rows]

    def along(dy, first, last):
        place = slice(first * rows, last * rows)
        return dot3(split(blocks(dy, first, last)), (rh[place, :], rl[place, :]), NN)

    def across(dz, first, last):
        turned = [blocks(dy, dz, dz + 1).T for dy in range(first, last)]
        turned = turned[0] if len(turned) == 1 else jnp.concatenate(turned, axis=1)
        place = slice(first * rows, last * rows)
        return dot3(split(turned), (lh[place, :], ll[place, :]), NN)

    to_y1[...] = along(1, 0, 4)
    to_z1[...] = across(1, 0, 3)
    to_y2[...] = along(2, 1, 3)
    to_z2[...] = across(2, 1, 2)
    to_z3[...] = across(3, 1, 2)
    to_own[...] = along(0, 0, 3) + across(0, 1, 3)


def product_part(where, scale, shares, own, near):
    rows, depth = own.shape
    out = jax.ShapeDtypeStruct((rows, depth), F32)
    return call(
        product_kernel,
        [out] * 6,
        [where, scale, *shares, own, *near],
        [pltpu.VMEM((rows, sum(KEPT) * rows), F32)]
        + [pltpu.VMEM((4 * rows, depth), BF16)] * 2
        + [pltpu.VMEM((3 * rows, depth), BF16)] * 2,
        flops=6 * 16 * rows * rows * depth,
        n_scalars=2,
    )


def line(axis, shift):
    pairs = [(i, (i + shift) % 4) for i in range(4)]
    if axis == "x":
        spot = [0, 2, 1, 3]
        return ("xl", "xh"), [(spot[a], spot[b]) for a, b in pairs]
    return axis, pairs


def send(value, axis, shift):
    return lax.ppermute(value, *line(axis, shift))


def swap(value, axis):
    return lax.ppermute(value, axis, [(0, 1), (1, 0)])


def sum_over_x(give, keep):
    other = swap(give, "core")
    mine = keep[0] + other[0]
    for d in (2, 1, 3):
        mine = mine + send(keep[d] + other[d], "x", d)
    return mine


def on_device(features, codes, codebooks):
    core = lax.axis_index("core")
    xl = lax.axis_index("xl")
    x = lax.axis_index("xh") * 2 + xl
    where = jnp.stack([core, x]).astype(jnp.int32)

    table = jnp.swapaxes(codebooks, 1, 2).reshape(-1, codebooks.shape[1])
    def half(which, features):
        chosen = jnp.concatenate([where, which[None].astype(jnp.int32)])
        return covariance_part(chosen, features, codes, table)

    give, keep = half(1 - xl, features)
    theirs, features = lax.optimization_barrier((keep + swap(give, "core"), features))
    theirs = swap(theirs, "xl")
    give, keep = half(xl, features)
    middle = give.shape[0] // 2
    from_core = [swap(piece, "core") for piece in (give[:middle], give[middle:])]
    current = (keep + jnp.concatenate(from_core, axis=0)) + theirs
    dimensions = features.shape[1] * 16
    moves = (("y", 1), ("z", 1), ("z", -1), ("y", 2), ("z", 2))

    for sweep in range(ITERS):
        near = [send(current, axis, -d) for axis, d in moves]
        mine = sum_over_x(*gram_part(where, current, near))
        ours = [mine] + [send(mine, "x", -d) for d in (1, 2, 3)]
        if sweep == 0:
            squares = mine[:8, -128:]
            for bit in (1, 2):
                squares = squares + lax.ppermute(squares, "y", [(i, i ^ bit) for i in range(4)])
            ours[1], squares = lax.optimization_barrier((ours[1], squares))
            factor = start_scale * jnp.sqrt(dimensions / (jnp.sum(squares) + epsilon))
        else:
            factor = jnp.float32(1)
        shares = ours + [swap(piece, "core") for piece in ours]
        value, *pieces = product_part(where, factor[None], shares, current, near)
        for piece, (axis, d) in zip(pieces, moves):
            value = value + send(piece, axis, d)
        current = factor * (1.5 * current - 0.5 * value)

    rank = xl * 2 + core
    rows = current.shape[0] // 4
    width = current.shape[1]
    out = jnp.zeros((rows, 4 * width), F32)
    for d in range(4):
        piece = lax.dynamic_slice_in_dim(current, (rank ^ d) * rows, rows, 0)
        if d:
            piece = lax.ppermute(piece, ("xl", "core"), [(i, i ^ d) for i in range(4)])
        out = lax.dynamic_update_slice_in_dim(out, piece, (rank ^ d) * width, 1)
    return out


def solution(mesh):
    devices = mesh.devices.reshape(2, 2, 4, 4, 2)
    return jax.shard_map(
        on_device,
        mesh=Mesh(devices, AXES),
        in_specs=(
            P(("xl", "core"), ("z", "y")),
            P(("xl", "core"), "xh"),
            P("xh", None, None),
        ),
        out_specs=P(("z", "y", "xl", "core"), "xh"),
        check_vma=False,
    )
```

```python
import functools

import jax
import jax.numpy as jnp
from jax import lax
from jax.experimental import pallas as pl
from jax.experimental.pallas import tpu as pltpu
from jax.sharding import Mesh, PartitionSpec as P

ITERS = 2

epsilon = 1e-06
start_scale = 0.45

F32 = jnp.float32
BF16 = jnp.bfloat16
AXES = ("xl", "core", "z", "y", "xh")
VMEM_BYTES = 48 * 1024 * 1024

NN = (((1,), (0,)), ((), ()))
NT = (((1,), (1,)), ((), ()))


def split(value):
    high = value.astype(BF16)
    return high, (value - high.astype(F32)).astype(BF16)


def dot3(a, b, dims):
    dot = functools.partial(lax.dot_general, dimension_numbers=dims, preferred_element_type=F32)
    return dot(a[0], b[0]) + (dot(a[0], b[1]) + dot(a[1], b[0]))


def call(kernel, out_shape, operands, scratch=(), flops=0, n_scalars=1):
    vmem = pl.BlockSpec(memory_space=pltpu.VMEM)
    smem = pl.BlockSpec(memory_space=pltpu.SMEM)
    moved = sum(o.size * o.dtype.itemsize for o in operands)
    moved += sum(o.size * o.dtype.itemsize for o in out_shape)
    return pl.pallas_call(
        kernel,
        out_shape=out_shape,
        in_specs=[smem] * n_scalars + [vmem] * (len(operands) - n_scalars),
        out_specs=[vmem] * len(out_shape),
        scratch_shapes=scratch,
        compiler_params=pltpu.CompilerParams(vmem_limit_bytes=VMEM_BYTES),
        cost_estimate=pl.CostEstimate(flops=flops, bytes_accessed=moved, transcendentals=0),
    )(*operands)


def covariance_kernel(where, features, codes, table, give, keep, turned, index, rebuilt):
    core, half = where[0], where[2]
    samples, count = codes.shape[0], index.shape[0]
    turned[...] = features[...].astype(F32).T.astype(BF16)
    index[...] = codes[:, pl.ds(pl.multiple_of(half * count, count), count)].T
    groups = rebuilt.shape[0] // 16
    for place, out in enumerate((give, keep)):
        target = lax.rem(core + 1 + place, 2)
        for part in range(out.shape[1] // rebuilt.shape[0]):
            start = target * (out.shape[1] // 8) + part * (rebuilt.shape[0] // 8)

            def pair(step, carry):
                first = start + 2 * step
                rows = pl.ds(pl.multiple_of((half * count + first) * 8, 16), 16)
                words = table[rows, :].astype(F32)
                decoded = []
                for which in range(2):
                    low = words[8 * which : 8 * which + 8, :128]
                    high = words[8 * which : 8 * which + 8, 128:]
                    code = index[pl.ds(first + which, 1), :]
                    pieces = []
                    for block in range(samples // 128):
                        picked = jnp.broadcast_to(code[:, block * 128 : block * 128 + 128], (8, 128))
                        place_in = picked & 127
                        a = jnp.take_along_axis(low, place_in, axis=1, mode="promise_in_bounds")
                        b = jnp.take_along_axis(high, place_in, axis=1, mode="promise_in_bounds")
                        pieces.append(jnp.where(picked < 128, a, b))
                    decoded.append(jnp.concatenate(pieces, axis=1))
                rebuilt[pl.ds(pl.multiple_of(step * 16, 16), 16), :] = jnp.concatenate(
                    decoded, axis=0
                ).astype(BF16)
                return carry

            lax.fori_loop(0, groups, pair, 0, unroll=True)
            width = rebuilt.shape[0]
            out[:, part * width : part * width + width] = lax.dot_general(
                turned[...], rebuilt[...], NT, preferred_element_type=F32
            )


def covariance_part(where, features, codes, table):
    samples, rows = features.shape
    quarter = codes.shape[1] * 2
    out = jax.ShapeDtypeStruct((rows, quarter), F32)
    return call(
        covariance_kernel,
        [out, out],
        [where, features, codes, table],
        [
            pltpu.VMEM((rows, samples), BF16),
            pltpu.VMEM((codes.shape[1] // 2, samples), jnp.int32),
            pltpu.VMEM((256, samples), BF16),
        ],
    )


BLOCKS = 5


def share(where, step, which):
    return lax.rem(where[1] + step, 4) * 2 + lax.rem(where[0] + which, 2)


def stack(high, low, refs):
    start = 0
    for ref in refs:
        place = slice(start, start + ref.shape[0])
        high[place, :], low[place, :] = split(ref[...])
        start += ref.shape[0]


def squares_of(refs):
    rows, depth = refs[0].shape
    column = sum(jnp.sum((ref[...] ** 2).reshape(rows // 8, 8, depth), axis=0) for ref in refs)
    return jnp.sum(column.reshape(8, -1, 128), axis=1)


def hand_out(where, gram, squares, give, keep):
    piece, width = give.shape[1], gram.shape[1]
    for step in range(4):
        for which, out in ((0, keep), (1, give)):
            start = share(where, step, which) * piece
            out[step, :, :width] = gram[pl.ds(pl.multiple_of(start, 8), piece), :]
            out[step, :8, width:] = squares
            out[step, 8:, width:] = jnp.zeros((piece - 8, 128), F32)


def near_gram_kernel(where, own, y1, z1, z3, give, keep, rh, rl, gram):
    rows = own.shape[0]
    stack(rh, rl, (own, z1, z3))
    gram[:, : 2 * rows] = dot3(split(own[...]), (rh[: 2 * rows, :], rl[: 2 * rows, :]), NT)
    gram[:, 2 * rows :] = dot3(split(y1[...]), (rh[...], rl[...]), NT)
    hand_out(where, gram, squares_of((own, z1, z3)), give, keep)


def far_gram_kernel(where, own, y1, z1, y2, z2, give, keep, rh, rl, gram):
    rows = own.shape[0]
    stack(rh, rl, (own, z1, z2))
    last = rh[2 * rows :, :], rl[2 * rows :, :]
    gram[:, :rows] = dot3(split(own[...]), last, NT)
    gram[:, rows : 2 * rows] = dot3(split(y1[...]), last, NT)
    gram[:, 2 * rows :] = dot3(split(y2[...]), (rh[...], rl[...]), NT)
    hand_out(where, gram, squares_of((z2,)), give, keep)


def gram_part(kernel, where, *pieces):
    rows, depth = pieces[0].shape
    width = BLOCKS * rows
    out = jax.ShapeDtypeStruct((4, rows // 8, width + 128), F32)
    return call(
        kernel,
        [out, out],
        [where, *pieces],
        [pltpu.VMEM((3 * rows, depth), BF16)] * 2 + [pltpu.VMEM((rows, width), F32)],
        flops=6 * rows * width * depth,
    )


def collect(where, scale, shares, gram):
    factor = scale[0]
    factor = factor * factor
    for step in range(4):
        for which in range(2):
            value = shares[4 * which + step][:, : gram.shape[1]] * factor
            start = share(where, step, which) * value.shape[0]
            gram[pl.ds(pl.multiple_of(start, 8), value.shape[0]), :] = value


def along(gram, first, last):
    rows = gram.shape[0]
    return gram[:, first * rows : last * rows]


def across(gram, *blocks):
    turned = [along(gram, block, block + 1).T for block in blocks]
    return turned[0] if len(turned) == 1 else jnp.concatenate(turned, axis=1)


def times(left, high, low, first, last):
    rows = left.shape[0]
    place = slice(first * rows, last * rows)
    return dot3(split(left), (high[place, :], low[place, :]), NN)


def near_product_kernel(where, scale, *refs):
    shares, (own, y1, z1, z3) = refs[:8], refs[8:12]
    to_own, to_y1, to_z1, to_z3, gram, high, low = refs[12:]
    collect(where, scale, shares, gram)
    stack(high, low, (y1, own, z1, z3))
    to_z3[...] = times(across(gram, 4), high, low, 0, 1)
    to_y1[...] = times(along(gram, 2, 5), high, low, 1, 4)
    to_z1[...] = times(across(gram, 3, 1), high, low, 0, 2)
    to_own[...] = times(along(gram, 0, 2), high, low, 1, 3) + times(
        across(gram, 2), high, low, 0, 1
    )


def far_product_kernel(where, scale, *refs):
    shares, (y1, z1, y2, z2), (part_own, part_y1, part_z1) = refs[:8], refs[8:12], refs[12:15]
    to_own, to_y1, to_z1, to_y2, to_z2, gram, high, low = refs[15:]
    collect(where, scale, shares, gram)
    stack(high, low, (y1, y2, z1, z2))
    to_y2[...] = times(along(gram, 3, 5), high, low, 2, 4)
    to_z2[...] = times(across(gram, 1), high, low, 0, 1)
    to_y1[...] = part_y1[...] + times(along(gram, 1, 2), high, low, 3, 4)
    to_z1[...] = part_z1[...] + times(across(gram, 3), high, low, 1, 2)
    to_own[...] = part_own[...] + (
        times(along(gram, 0, 1), high, low, 3, 4) + times(across(gram, 2), high, low, 1, 2)
    )


def product_part(kernel, count, flops, where, scale, shares, *pieces):
    rows, depth = pieces[0].shape
    return call(
        kernel,
        [jax.ShapeDtypeStruct((rows, depth), F32)] * count,
        [where, scale, *shares, *pieces],
        [pltpu.VMEM((rows, BLOCKS * rows), F32)] + [pltpu.VMEM((4 * rows, depth), BF16)] * 2,
        flops=6 * flops * rows * rows * depth,
        n_scalars=2,
    )


def line(axis, shift):
    pairs = [(i, (i + shift) % 4) for i in range(4)]
    if axis == "x":
        spot = [0, 2, 1, 3]
        return ("xl", "xh"), [(spot[a], spot[b]) for a, b in pairs]
    return axis, pairs


def send(value, axis, shift):
    return lax.ppermute(value, *line(axis, shift))


def swap(value, axis):
    return lax.ppermute(value, axis, [(0, 1), (1, 0)])


def core_sum(give, keep):
    other = swap(give, "core")
    return [keep[d] + other[d] for d in range(4)]


def send_over_x(parts):
    return [parts[0]] + [send(parts[d], "x", d) for d in (2, 1, 3)]


def after(value, *others):
    return lax.optimization_barrier((value, others))[0]


def own_chips(mine):
    return [mine] + [send(mine, "x", -d) for d in (1, 2, 3)]


def spread_over_x(mine):
    ours = own_chips(mine)
    return ours + [swap(piece, "core") for piece in ours]


def on_device(features, codes, codebooks):
    core = lax.axis_index("core")
    xl = lax.axis_index("xl")
    x = lax.axis_index("xh") * 2 + xl
    where = jnp.stack([core, x]).astype(jnp.int32)

    table = jnp.swapaxes(codebooks, 1, 2).reshape(-1, codebooks.shape[1])
    def half(which, features):
        chosen = jnp.concatenate([where, which[None].astype(jnp.int32)])
        return covariance_part(chosen, features, codes, table)

    give, keep = half(1 - xl, features)
    theirs, features = lax.optimization_barrier((keep + swap(give, "core"), features))
    theirs = swap(theirs, "xl")
    give, keep = half(xl, features)
    middle = give.shape[0] // 2
    from_core = [swap(piece, "core") for piece in (give[:middle], give[middle:])]
    current = (keep + jnp.concatenate(from_core, axis=0)) + theirs
    dimensions = features.shape[1] * 16
    for sweep in range(ITERS):
        y1, z1, z3 = [send(current, axis, -d) for axis, d in (("y", 1), ("z", 1), ("z", -1))]
        y2, z2 = send(current, "y", 2), send(current, "z", 2)
        y1, z1, z3, y2, z2 = lax.optimization_barrier((y1, z1, z3, y2, z2))
        parts = core_sum(*gram_part(near_gram_kernel, where, current, y1, z1, z3))
        addends = send_over_x(parts)
        y1_later = after(y1, *parts)
        give, keep = gram_part(far_gram_kernel, where, current, y1_later, z1, y2, z2)
        addends, give = lax.optimization_barrier((addends, give))
        near_mine = sum(addends[1:], addends[0])
        near_shares = spread_over_x(near_mine)
        addends = send_over_x(core_sum(give, keep))
        far_mine = sum(addends[1:], addends[0])
        ours = own_chips(far_mine)
        if sweep == 0:
            squares = near_mine[:8, -128:] + far_mine[:8, -128:]
            for bit in (1, 2):
                squares = squares + lax.ppermute(squares, "y", [(i, i ^ bit) for i in range(4)])
            ours[1], squares = lax.optimization_barrier((ours[1], squares))
            factor = start_scale * jnp.sqrt(dimensions / (jnp.sum(squares) + epsilon))
        else:
            factor = jnp.float32(1)
        far_shares = ours + [swap(piece, "core") for piece in ours]
        value, to_y1, to_z1, to_z3 = product_part(
            near_product_kernel, 4, 9, where, factor[None], near_shares, current, y1, z1, z3
        )
        value, to_y1, to_z1, to_y2, to_z2 = product_part(
            far_product_kernel, 5, 7, where, factor[None], far_shares,
            y1, z1, y2, z2, value, to_y1, to_z1,
        )
        for piece, axis, d in (
            (to_z3, "z", -1),
            (to_y1, "y", 1),
            (to_z1, "z", 1),
            (to_y2, "y", 2),
            (to_z2, "z", 2),
        ):
            value = value + send(piece, axis, d)
        current = factor * (1.5 * current - 0.5 * value)

    rank = xl * 2 + core
    rows = current.shape[0] // 4
    width = current.shape[1]
    out = jnp.zeros((rows, 4 * width), F32)
    for d in range(4):
        piece = lax.dynamic_slice_in_dim(current, (rank ^ d) * rows, rows, 0)
        if d:
            piece = lax.ppermute(piece, ("xl", "core"), [(i, i ^ d) for i in range(4)])
        out = lax.dynamic_update_slice_in_dim(out, piece, (rank ^ d) * width, 1)
    return out


def solution(mesh):
    devices = mesh.devices.reshape(2, 2, 4, 4, 2)
    return jax.shard_map(
        on_device,
        mesh=Mesh(devices, AXES),
        in_specs=(
            P(("xl", "core"), ("z", "y")),
            P(("xl", "core"), "xh"),
            P("xh", None, None),
        ),
        out_specs=P(("z", "y", "xl", "core"), "xh"),
        check_vma=False,
    )
```

```python
import functools

import jax
import jax.numpy as jnp
from jax import lax
from jax.experimental import pallas as pl
from jax.experimental.pallas import tpu as pltpu
from jax.sharding import Mesh, PartitionSpec as P

ITERS = 2

epsilon = 1e-06
start_scale = 0.45

F32 = jnp.float32
BF16 = jnp.bfloat16
AXES = ("xl", "core", "z", "y", "xh")
VMEM_BYTES = 48 * 1024 * 1024

NN = (((1,), (0,)), ((), ()))
NT = (((1,), (1,)), ((), ()))


def split(value):
    high = value.astype(BF16)
    return high, (value - high.astype(F32)).astype(BF16)


def dot3(a, b, dims):
    dot = functools.partial(lax.dot_general, dimension_numbers=dims, preferred_element_type=F32)
    return dot(a[0], b[0]) + (dot(a[0], b[1]) + dot(a[1], b[0]))


def call(kernel, out_shape, operands, scratch=(), flops=0, n_scalars=1):
    vmem = pl.BlockSpec(memory_space=pltpu.VMEM)
    smem = pl.BlockSpec(memory_space=pltpu.SMEM)
    moved = sum(o.size * o.dtype.itemsize for o in operands)
    moved += sum(o.size * o.dtype.itemsize for o in out_shape)
    return pl.pallas_call(
        kernel,
        out_shape=out_shape,
        in_specs=[smem] * n_scalars + [vmem] * (len(operands) - n_scalars),
        out_specs=[vmem] * len(out_shape),
        scratch_shapes=scratch,
        compiler_params=pltpu.CompilerParams(vmem_limit_bytes=VMEM_BYTES),
        cost_estimate=pl.CostEstimate(flops=flops, bytes_accessed=moved, transcendentals=0),
    )(*operands)


def covariance_kernel(where, features, codes, table, give, keep, turned, index, rebuilt):
    core, half = where[0], where[4]
    samples, count = codes.shape[0], index.shape[0]
    turned[...] = features[...].astype(F32).T.astype(BF16)
    index[...] = codes[:, pl.ds(pl.multiple_of(half * count, count), count)].T
    groups = rebuilt.shape[0] // 16
    for place, out in enumerate((give, keep)):
        target = lax.rem(core + 1 + place, 2)
        for part in range(out.shape[1] // rebuilt.shape[0]):
            start = target * (out.shape[1] // 8) + part * (rebuilt.shape[0] // 8)

            def pair(step, carry):
                first = start + 2 * step
                rows = pl.ds(pl.multiple_of((half * count + first) * 8, 16), 16)
                words = table[rows, :].astype(F32)
                decoded = []
                for which in range(2):
                    low = words[8 * which : 8 * which + 8, :128]
                    high = words[8 * which : 8 * which + 8, 128:]
                    code = index[pl.ds(first + which, 1), :]
                    pieces = []
                    for block in range(samples // 128):
                        picked = jnp.broadcast_to(code[:, block * 128 : block * 128 + 128], (8, 128))
                        place_in = picked & 127
                        a = jnp.take_along_axis(low, place_in, axis=1, mode="promise_in_bounds")
                        b = jnp.take_along_axis(high, place_in, axis=1, mode="promise_in_bounds")
                        pieces.append(jnp.where(picked < 128, a, b))
                    decoded.append(jnp.concatenate(pieces, axis=1))
                rebuilt[pl.ds(pl.multiple_of(step * 16, 16), 16), :] = jnp.concatenate(
                    decoded, axis=0
                ).astype(BF16)
                return carry

            lax.fori_loop(0, groups, pair, 0, unroll=True)
            width = rebuilt.shape[0]
            out[:, part * width : part * width + width] = lax.dot_general(
                turned[...], rebuilt[...], NT, preferred_element_type=F32
            )


def covariance_part(where, features, codes, table):
    samples, rows = features.shape
    quarter = codes.shape[1] * 2
    out = jax.ShapeDtypeStruct((rows, quarter), F32)
    return call(
        covariance_kernel,
        [out, out],
        [where, features, codes, table],
        [
            pltpu.VMEM((rows, samples), BF16),
            pltpu.VMEM((codes.shape[1] // 2, samples), jnp.int32),
            pltpu.VMEM((256, samples), BF16),
        ],
    )


OWN, Z1, Z2, Z3, Y2, Y1 = range(6)
WHOLE = 7
HALVES = ((OWN, Z2, 2), (OWN, Y2, 3), (Y2, Z2, 2))


def half_rows(where, u, v, side, rows):
    first = where[side] == 1
    left = jnp.where(first, u * rows, v * rows + rows // 2)
    right = jnp.where(first, v * rows, u * rows)
    return (
        pl.ds(pl.multiple_of(left, rows // 2), rows // 2),
        pl.ds(pl.multiple_of(right, rows), rows),
    )


def share(where, step, which):
    return lax.rem(where[1] + step, 4) * 2 + lax.rem(where[0] + which, 2)


def stack(high, low, refs):
    start = 0
    for ref in refs:
        place = slice(start, start + ref.shape[0])
        high[place, :], low[place, :] = split(ref[...])
        start += ref.shape[0]


def gram_kernel(where, own, z1, z3, y1, z2, y2, give, keep, high, low, gram):
    rows, depth = own.shape
    stack(high, low, (own, z1, z2, z3, y2))
    column = sum(
        jnp.sum((ref[...] ** 2).reshape(rows // 8, 8, depth), axis=0) for ref in (own, z1, z2, z3)
    )
    squares = jnp.sum(column.reshape(8, -1, 128), axis=1)

    def pieces(first, last):
        return high[first * rows : last * rows, :], low[first * rows : last * rows, :]

    gram[:, : 2 * rows] = dot3(pieces(OWN, OWN + 1), pieces(OWN, Z1 + 1), NT)
    gram[:, 2 * rows : 6 * rows] = dot3(split(y1[...]), pieces(OWN, Z3 + 1), NT)
    gram[:, 6 * rows : 7 * rows] = dot3(pieces(Y2, Y2 + 1), pieces(Z1, Z1 + 1), NT)
    half, start = rows // 2, WHOLE * rows
    for u, v, side in HALVES:
        left, right = half_rows(where, u, v, side, rows)
        value = dot3((high[left, :], low[left, :]), (high[right, :], low[right, :]), NT)
        gram[:half, start : start + half] = value[:, :half]
        gram[half:, start : start + half] = value[:, half:]
        start += half
    piece, width = rows // 8, gram.shape[1]
    for step in range(4):
        for which, out in ((0, keep), (1, give)):
            place = share(where, step, which) * piece
            out[step, :, :width] = gram[pl.ds(pl.multiple_of(place, 8), piece), :]
            out[step, :8, width:] = squares
            out[step, 8:, width:] = jnp.zeros((piece - 8, 128), F32)


def gram_width(rows):
    return WHOLE * rows + len(HALVES) * rows // 2


def gram_part(where, own, near):
    rows, depth = own.shape
    width = gram_width(rows)
    out = jax.ShapeDtypeStruct((4, rows // 8, width + 128), F32)
    return call(
        gram_kernel,
        [out, out],
        [where, own, *near],
        [pltpu.VMEM((5 * rows, depth), BF16)] * 2 + [pltpu.VMEM((rows, width), F32)],
        flops=6 * rows * width * depth,
    )


def collect(where, scale, shares, gram):
    factor = scale[0]
    factor = factor * factor
    for step in range(4):
        for which in range(2):
            value = shares[4 * which + step][:, : gram.shape[1]] * factor
            start = share(where, step, which) * value.shape[0]
            gram[pl.ds(pl.multiple_of(start, 8), value.shape[0]), :] = value


def along(gram, first, last):
    rows = gram.shape[0]
    return gram[:, first * rows : last * rows]


def across(gram, *blocks):
    turned = [along(gram, block, block + 1).T for block in blocks]
    return turned[0] if len(turned) == 1 else jnp.concatenate(turned, axis=1)


def times(left, high, low, first, last):
    rows = left.shape[0]
    place = slice(first * rows, last * rows)
    return dot3(split(left), (high[place, :], low[place, :]), NN)


def near_product_kernel(where, scale, *refs):
    shares, (own, z1, z3, y1, z2, y2), (to_z1, to_z3, to_y1) = refs[:8], refs[8:14], refs[14:17]
    gram, high, low = refs[17:]
    collect(where, scale, shares, gram)
    stack(high, low, (own, z1, z2, z3, y2, y1))
    to_z1[...] = times(across(gram, 6, 3), high, low, Y2, Y1 + 1) + times(
        across(gram, 1), high, low, OWN, OWN + 1
    )
    to_z3[...] = times(across(gram, 5), high, low, Y1, Y1 + 1)
    to_y1[...] = times(along(gram, 2, 6), high, low, OWN, Z3 + 1)


def far_product_kernel(where, scale, *refs):
    shares, (own, z1, z3, y1, z2, y2), (to_own, to_z2, to_y2) = refs[:8], refs[8:14], refs[14:17]
    gram, high, low, sums = refs[17:]
    rows = own.shape[0]
    collect(where, scale, shares, gram)
    stack(high, low, (own, z1, z2, z3, y2, y1))

    def sum_of(place):
        return sums.at[place * rows : place * rows + rows, :]

    sum_of(OWN)[...] = times(along(gram, 0, 2), high, low, OWN, Z1 + 1) + times(
        across(gram, 2), high, low, Y1, Y1 + 1
    )
    sum_of(Z2)[...] = times(across(gram, 4), high, low, Y1, Y1 + 1)
    sum_of(Y2)[...] = times(along(gram, 6, 7), high, low, Z1, Z1 + 1)
    half, start = rows // 2, WHOLE * rows
    for u, v, side in HALVES:
        left, right = half_rows(where, u, v, side, rows)
        folded = gram[:, start : start + half]
        value = jnp.concatenate([folded[:half, :], folded[half:, :]], axis=1)
        sums[left, :] += dot3(split(value), (high[right, :], low[right, :]), NN)
        sums[right, :] += dot3(split(value.T), (high[left, :], low[left, :]), NN)
        start += half
    to_own[...] = sum_of(OWN)[...]
    to_z2[...] = sum_of(Z2)[...]
    to_y2[...] = sum_of(Y2)[...]


def product_part(kernel, where, scale, shares, *pieces):
    rows, depth = pieces[0].shape
    scratch = [pltpu.VMEM((rows, gram_width(rows)), F32)]
    scratch += [pltpu.VMEM((6 * rows, depth), BF16)] * 2
    if kernel is far_product_kernel:
        scratch.append(pltpu.VMEM((5 * rows, depth), F32))
    return call(
        kernel,
        [jax.ShapeDtypeStruct((rows, depth), F32)] * 3,
        [where, scale, *shares, *pieces],
        scratch,
        flops=6 * 8 * rows * rows * depth,
        n_scalars=2,
    )


def line(axis, shift):
    pairs = [(i, (i + shift) % 4) for i in range(4)]
    if axis == "x":
        spot = [0, 2, 1, 3]
        return ("xl", "xh"), [(spot[a], spot[b]) for a, b in pairs]
    return axis, pairs


def send(value, axis, shift):
    return lax.ppermute(value, *line(axis, shift))


def swap(value, axis):
    return lax.ppermute(value, axis, [(0, 1), (1, 0)])


def sum_over_x(give, keep):
    other = swap(give, "core")
    mine = keep[0] + other[0]
    for d in (2, 1, 3):
        mine = mine + send(keep[d] + other[d], "x", d)
    return mine


def on_device(features, codes, codebooks):
    core = lax.axis_index("core")
    xl = lax.axis_index("xl")
    x = lax.axis_index("xh") * 2 + xl
    sides = [lax.axis_index(axis) < 2 for axis in ("z", "y")]
    where = jnp.stack([core, x, *sides]).astype(jnp.int32)

    table = jnp.swapaxes(codebooks, 1, 2).reshape(-1, codebooks.shape[1])
    def half(which, features):
        chosen = jnp.concatenate([where, which[None].astype(jnp.int32)])
        return covariance_part(chosen, features, codes, table)

    give, keep = half(1 - xl, features)
    theirs, features = lax.optimization_barrier((keep + swap(give, "core"), features))
    theirs = swap(theirs, "xl")
    give, keep = half(xl, features)
    middle = give.shape[0] // 2
    from_core = [swap(piece, "core") for piece in (give[:middle], give[middle:])]
    current = (keep + jnp.concatenate(from_core, axis=0)) + theirs
    dimensions = features.shape[1] * 16
    moves = (("z", 1), ("z", -1), ("y", 1), ("z", 2), ("y", 2))

    for sweep in range(ITERS):
        near = [send(current, axis, -d) for axis, d in moves]
        mine = sum_over_x(*gram_part(where, current, near))
        ours = [mine] + [send(mine, "x", -d) for d in (1, 2, 3)]
        if sweep == 0:
            squares = mine[:8, -128:]
            for bit in (1, 2):
                squares = squares + lax.ppermute(squares, "y", [(i, i ^ bit) for i in range(4)])
            ours[1], squares = lax.optimization_barrier((ours[1], squares))
            factor = start_scale * jnp.sqrt(dimensions / (jnp.sum(squares) + epsilon))
        else:
            factor = jnp.float32(1)
        shares = ours + [swap(piece, "core") for piece in ours]
        given = where, factor[None], shares, current, *near
        pieces = product_part(near_product_kernel, *given)
        value, *far_pieces = product_part(far_product_kernel, *given)
        for piece, (axis, d) in zip((*pieces, *far_pieces), moves):
            value = value + send(piece, axis, d)
        current = factor * (1.5 * current - 0.5 * value)

    rank = xl * 2 + core
    rows = current.shape[0] // 4
    width = current.shape[1]
    out = jnp.zeros((rows, 4 * width), F32)
    for d in range(4):
        piece = lax.dynamic_slice_in_dim(current, (rank ^ d) * rows, rows, 0)
        if d:
            piece = lax.ppermute(piece, ("xl", "core"), [(i, i ^ d) for i in range(4)])
        out = lax.dynamic_update_slice_in_dim(out, piece, (rank ^ d) * width, 1)
    return out


def solution(mesh):
    devices = mesh.devices.reshape(2, 2, 4, 4, 2)
    return jax.shard_map(
        on_device,
        mesh=Mesh(devices, AXES),
        in_specs=(
            P(("xl", "core"), ("z", "y")),
            P(("xl", "core"), "xh"),
            P("xh", None, None),
        ),
        out_specs=P(("z", "y", "xl", "core"), "xh"),
        check_vma=False,
    )
```

```python
import functools

import jax
import jax.numpy as jnp
from jax import lax
from jax.experimental import pallas as pl
from jax.experimental.pallas import tpu as pltpu
from jax.sharding import Mesh, PartitionSpec as P

ITERS = 2

epsilon = 1e-06
start_scale = 0.45

F32 = jnp.float32
BF16 = jnp.bfloat16
AXES = ("xl", "core", "z", "y", "xh")
VMEM_BYTES = 48 * 1024 * 1024

NN = (((1,), (0,)), ((), ()))
NT = (((1,), (1,)), ((), ()))


def split(value):
    high = value.astype(BF16)
    return high, (value - high.astype(F32)).astype(BF16)


def dot3(a, b, dims):
    dot = functools.partial(lax.dot_general, dimension_numbers=dims, preferred_element_type=F32)
    return dot(a[0], b[0]) + (dot(a[0], b[1]) + dot(a[1], b[0]))


def call(kernel, out_shape, operands, scratch=(), flops=0, n_scalars=1):
    vmem = pl.BlockSpec(memory_space=pltpu.VMEM)
    smem = pl.BlockSpec(memory_space=pltpu.SMEM)
    moved = sum(o.size * o.dtype.itemsize for o in operands)
    moved += sum(o.size * o.dtype.itemsize for o in out_shape)
    return pl.pallas_call(
        kernel,
        out_shape=out_shape,
        in_specs=[smem] * n_scalars + [vmem] * (len(operands) - n_scalars),
        out_specs=[vmem] * len(out_shape),
        scratch_shapes=scratch,
        compiler_params=pltpu.CompilerParams(vmem_limit_bytes=VMEM_BYTES),
        cost_estimate=pl.CostEstimate(flops=flops, bytes_accessed=moved, transcendentals=0),
    )(*operands)


def covariance_kernel(where, features, codes, table, give, keep, turned, index, rebuilt):
    core, half = where[0], where[4]
    samples, count = codes.shape[0], index.shape[0]
    turned[...] = features[...].astype(F32).T.astype(BF16)
    index[...] = codes[:, pl.ds(pl.multiple_of(half * count, count), count)].T
    parts, width, _ = rebuilt.shape
    quarter = give.shape[1] // 8

    def decode(part, carry):
        target = lax.rem(core + 1 + part // 2, 2)
        start = target * quarter + lax.rem(part, 2) * (width // 8)
        for step in range(width // 16):
            first = start + 2 * step
            rows = pl.ds(pl.multiple_of((half * count + first) * 8, 16), 16)
            words = table[rows, :].astype(F32)
            decoded = []
            for which in range(2):
                low = words[8 * which : 8 * which + 8, :128]
                high = words[8 * which : 8 * which + 8, 128:]
                code = index[pl.ds(first + which, 1), :]
                pieces = []
                for block in range(samples // 128):
                    picked = jnp.broadcast_to(code[:, block * 128 : block * 128 + 128], (8, 128))
                    place = picked & 127
                    a = jnp.take_along_axis(low, place, axis=1, mode="promise_in_bounds")
                    b = jnp.take_along_axis(high, place, axis=1, mode="promise_in_bounds")
                    pieces.append(jnp.where(picked < 128, a, b))
                decoded.append(jnp.concatenate(pieces, axis=1))
            rebuilt[part, step * 16 : step * 16 + 16, :] = jnp.concatenate(decoded, axis=0).astype(
                BF16
            )
        return carry

    lax.fori_loop(0, parts, decode, 0)
    for part in range(parts):
        out = (give, keep)[part // 2]
        start = (part % 2) * width
        out[:, start : start + width] = lax.dot_general(
            turned[...], rebuilt[part], NT, preferred_element_type=F32
        )


def covariance_part(where, features, codes, table):
    samples, rows = features.shape
    quarter = codes.shape[1] * 2
    out = jax.ShapeDtypeStruct((rows, quarter), F32)
    return call(
        covariance_kernel,
        [out, out],
        [where, features, codes, table],
        [
            pltpu.VMEM((rows, samples), BF16),
            pltpu.VMEM((codes.shape[1] // 2, samples), jnp.int32),
            pltpu.VMEM((4, quarter // 2, samples), BF16),
        ],
    )


OWN, Z1, Z2, Z3, Y2, Y1 = range(6)
WHOLE = 7
HALVES = ((OWN, Z2, 2), (OWN, Y2, 3), (Y2, Z2, 2))


def half_rows(where, u, v, side, rows):
    first = where[side] == 1
    left = jnp.where(first, u * rows, v * rows + rows // 2)
    right = jnp.where(first, v * rows, u * rows)
    return (
        pl.ds(pl.multiple_of(left, rows // 2), rows // 2),
        pl.ds(pl.multiple_of(right, rows), rows),
    )


def share(where, step, which):
    return lax.rem(where[1] + step, 4) * 2 + lax.rem(where[0] + which, 2)


def stack(high, low, refs):
    start = 0
    for ref in refs:
        place = slice(start, start + ref.shape[0])
        high[place, :], low[place, :] = split(ref[...])
        start += ref.shape[0]


def gram_kernel(where, own, z1, z3, y1, z2, y2, give, keep, high, low, gram):
    rows, depth = own.shape
    stack(high, low, (own, z1, z2, z3, y2))
    column = sum(
        jnp.sum((ref[...] ** 2).reshape(rows // 8, 8, depth), axis=0) for ref in (own, z1, z2, z3)
    )
    squares = jnp.sum(column.reshape(8, -1, 128), axis=1)

    def pieces(first, last):
        return high[first * rows : last * rows, :], low[first * rows : last * rows, :]

    gram[:, : 2 * rows] = dot3(pieces(OWN, OWN + 1), pieces(OWN, Z1 + 1), NT)
    gram[:, 2 * rows : 6 * rows] = dot3(split(y1[...]), pieces(OWN, Z3 + 1), NT)
    gram[:, 6 * rows : 7 * rows] = dot3(pieces(Y2, Y2 + 1), pieces(Z1, Z1 + 1), NT)
    half, start = rows // 2, WHOLE * rows
    for u, v, side in HALVES:
        left, right = half_rows(where, u, v, side, rows)
        value = dot3((high[left, :], low[left, :]), (high[right, :], low[right, :]), NT)
        gram[:half, start : start + half] = value[:, :half]
        gram[half:, start : start + half] = value[:, half:]
        start += half
    piece, width = rows // 8, gram.shape[1]
    for step in range(4):
        for which, out in ((0, keep), (1, give)):
            place = share(where, step, which) * piece
            out[step, :, :width] = gram[pl.ds(pl.multiple_of(place, 8), piece), :]
            out[step, :8, width:] = squares
            out[step, 8:, width:] = jnp.zeros((piece - 8, 128), F32)


def gram_width(rows):
    return WHOLE * rows + len(HALVES) * rows // 2


def gram_part(where, own, near):
    rows, depth = own.shape
    width = gram_width(rows)
    out = jax.ShapeDtypeStruct((4, rows // 8, width + 128), F32)
    return call(
        gram_kernel,
        [out, out],
        [where, own, *near],
        [pltpu.VMEM((5 * rows, depth), BF16)] * 2 + [pltpu.VMEM((rows, width), F32)],
        flops=6 * rows * width * depth,
    )


def collect(where, scale, shares, gram):
    factor = scale[0]
    factor = factor * factor
    for step in range(4):
        for which in range(2):
            value = shares[4 * which + step][:, : gram.shape[1]] * factor
            start = share(where, step, which) * value.shape[0]
            gram[pl.ds(pl.multiple_of(start, 8), value.shape[0]), :] = value


def along(gram, first, last):
    rows = gram.shape[0]
    return gram[:, first * rows : last * rows]


def across(gram, *blocks):
    turned = [along(gram, block, block + 1).T for block in blocks]
    return turned[0] if len(turned) == 1 else jnp.concatenate(turned, axis=1)


def times(left, high, low, first, last):
    rows = left.shape[0]
    place = slice(first * rows, last * rows)
    return dot3(split(left), (high[place, :], low[place, :]), NN)


def near_product_kernel(where, scale, *refs):
    shares, (own, z1, z3, y1, z2, y2), (to_z1, to_z3, to_y1) = refs[:8], refs[8:14], refs[14:17]
    gram, high, low = refs[17:]
    collect(where, scale, shares, gram)
    stack(high, low, (own, z1, z2, z3, y2, y1))
    to_z1[...] = times(across(gram, 6, 3), high, low, Y2, Y1 + 1) + times(
        across(gram, 1), high, low, OWN, OWN + 1
    )
    to_z3[...] = times(across(gram, 5), high, low, Y1, Y1 + 1)
    to_y1[...] = times(along(gram, 2, 6), high, low, OWN, Z3 + 1)


def far_product_kernel(where, scale, *refs):
    shares, (own, z1, z3, y1, z2, y2), (to_own, to_z2, to_y2) = refs[:8], refs[8:14], refs[14:17]
    gram, high, low, sums = refs[17:]
    rows = own.shape[0]
    collect(where, scale, shares, gram)
    stack(high, low, (own, z1, z2, z3, y2, y1))

    def sum_of(place):
        return sums.at[place * rows : place * rows + rows, :]

    sum_of(OWN)[...] = times(along(gram, 0, 2), high, low, OWN, Z1 + 1) + times(
        across(gram, 2), high, low, Y1, Y1 + 1
    )
    sum_of(Z2)[...] = times(across(gram, 4), high, low, Y1, Y1 + 1)
    sum_of(Y2)[...] = times(along(gram, 6, 7), high, low, Z1, Z1 + 1)
    half, start = rows // 2, WHOLE * rows
    for u, v, side in HALVES:
        left, right = half_rows(where, u, v, side, rows)
        folded = gram[:, start : start + half]
        value = jnp.concatenate([folded[:half, :], folded[half:, :]], axis=1)
        sums[left, :] += dot3(split(value), (high[right, :], low[right, :]), NN)
        sums[right, :] += dot3(split(value.T), (high[left, :], low[left, :]), NN)
        start += half
    to_own[...] = sum_of(OWN)[...]
    to_z2[...] = sum_of(Z2)[...]
    to_y2[...] = sum_of(Y2)[...]


def product_part(kernel, where, scale, shares, *pieces):
    rows, depth = pieces[0].shape
    scratch = [pltpu.VMEM((rows, gram_width(rows)), F32)]
    scratch += [pltpu.VMEM((6 * rows, depth), BF16)] * 2
    if kernel is far_product_kernel:
        scratch.append(pltpu.VMEM((5 * rows, depth), F32))
    return call(
        kernel,
        [jax.ShapeDtypeStruct((rows, depth), F32)] * 3,
        [where, scale, *shares, *pieces],
        scratch,
        flops=6 * 8 * rows * rows * depth,
        n_scalars=2,
    )


def line(axis, shift):
    pairs = [(i, (i + shift) % 4) for i in range(4)]
    if axis == "x":
        spot = [0, 2, 1, 3]
        return ("xl", "xh"), [(spot[a], spot[b]) for a, b in pairs]
    return axis, pairs


def send(value, axis, shift):
    return lax.ppermute(value, *line(axis, shift))


def swap(value, axis):
    return lax.ppermute(value, axis, [(0, 1), (1, 0)])


def sum_over_x(give, keep):
    other = swap(give, "core")
    mine = keep[0] + other[0]
    for d in (2, 1, 3):
        mine = mine + send(keep[d] + other[d], "x", d)
    return mine


def on_device(features, codes, codebooks):
    core = lax.axis_index("core")
    xl = lax.axis_index("xl")
    x = lax.axis_index("xh") * 2 + xl
    sides = [lax.axis_index(axis) < 2 for axis in ("z", "y")]
    where = jnp.stack([core, x, *sides]).astype(jnp.int32)

    table = jnp.swapaxes(codebooks, 1, 2).reshape(-1, codebooks.shape[1])
    def half(which, features):
        chosen = jnp.concatenate([where, which[None].astype(jnp.int32)])
        return covariance_part(chosen, features, codes, table)

    give, keep = half(1 - xl, features)
    theirs, features = lax.optimization_barrier((keep + swap(give, "core"), features))
    theirs = swap(theirs, "xl")
    give, keep = half(xl, features)
    middle = give.shape[0] // 2
    from_core = [swap(piece, "core") for piece in (give[:middle], give[middle:])]
    current = (keep + jnp.concatenate(from_core, axis=0)) + theirs
    dimensions = features.shape[1] * 16
    moves = (("z", 1), ("z", -1), ("y", 1), ("z", 2), ("y", 2))

    for sweep in range(ITERS):
        near = [send(current, axis, -d) for axis, d in moves]
        mine = sum_over_x(*gram_part(where, current, near))
        ours = [mine] + [send(mine, "x", -d) for d in (1, 2, 3)]
        if sweep == 0:
            squares = mine[:8, -128:]
            for bit in (1, 2):
                squares = squares + lax.ppermute(squares, "y", [(i, i ^ bit) for i in range(4)])
            ours[1], squares = lax.optimization_barrier((ours[1], squares))
            factor = start_scale * jnp.sqrt(dimensions / (jnp.sum(squares) + epsilon))
        else:
            factor = jnp.float32(1)
        shares = ours + [swap(piece, "core") for piece in ours]
        given = where, factor[None], shares, current, *near
        pieces = product_part(near_product_kernel, *given)
        value, *far_pieces = product_part(far_product_kernel, *given)
        for piece, (axis, d) in zip((*pieces, *far_pieces), moves):
            value = value + send(piece, axis, d)
        current = factor * (1.5 * current - 0.5 * value)

    rank = xl * 2 + core
    rows = current.shape[0] // 4
    width = current.shape[1]
    out = jnp.zeros((rows, 4 * width), F32)
    for d in range(4):
        piece = lax.dynamic_slice_in_dim(current, (rank ^ d) * rows, rows, 0)
        if d:
            piece = lax.ppermute(piece, ("xl", "core"), [(i, i ^ d) for i in range(4)])
        out = lax.dynamic_update_slice_in_dim(out, piece, (rank ^ d) * width, 1)
    return out


def solution(mesh):
    devices = mesh.devices.reshape(2, 2, 4, 4, 2)
    return jax.shard_map(
        on_device,
        mesh=Mesh(devices, AXES),
        in_specs=(
            P(("xl", "core"), ("z", "y")),
            P(("xl", "core"), "xh"),
            P("xh", None, None),
        ),
        out_specs=P(("z", "y", "xl", "core"), "xh"),
        check_vma=False,
    )
```

```python
import functools

import jax
import jax.numpy as jnp
from jax import lax
from jax.experimental import pallas as pl
from jax.experimental.pallas import tpu as pltpu
from jax.sharding import Mesh, PartitionSpec as P

ITERS = 2

epsilon = 1e-06
start_scale = 0.45

F32 = jnp.float32
BF16 = jnp.bfloat16
AXES = ("xl", "core", "z", "y", "xh")
VMEM_BYTES = 32 * 1024 * 1024

NN = (((1,), (0,)), ((), ()))
NT = (((1,), (1,)), ((), ()))


def split(value):
    high = value.astype(BF16)
    return high, (value - high.astype(F32)).astype(BF16)


def dot3(a, b, dims):
    dot = functools.partial(lax.dot_general, dimension_numbers=dims, preferred_element_type=F32)
    return dot(a[0], b[0]) + (dot(a[0], b[1]) + dot(a[1], b[0]))


def call(kernel, out_shape, operands, scratch=(), flops=0, n_scalars=1):
    vmem = pl.BlockSpec(memory_space=pltpu.VMEM)
    smem = pl.BlockSpec(memory_space=pltpu.SMEM)
    moved = sum(o.size * o.dtype.itemsize for o in operands)
    moved += sum(o.size * o.dtype.itemsize for o in out_shape)
    return pl.pallas_call(
        kernel,
        out_shape=out_shape,
        in_specs=[smem] * n_scalars + [vmem] * (len(operands) - n_scalars),
        out_specs=[vmem] * len(out_shape),
        scratch_shapes=scratch,
        compiler_params=pltpu.CompilerParams(vmem_limit_bytes=VMEM_BYTES),
        cost_estimate=pl.CostEstimate(flops=flops, bytes_accessed=moved, transcendentals=0),
    )(*operands)


def covariance_kernel(where, features, codes, table, give, keep, turned, index, rebuilt):
    core, half = where[0], where[4]
    samples, count = codes.shape[0], index.shape[0]
    turned[...] = features[...].astype(F32).T.astype(BF16)
    index[...] = codes[:, pl.ds(pl.multiple_of(half * count, count), count)].T
    parts, width, _ = rebuilt.shape
    quarter = give.shape[1] // 8

    def decode(part, carry):
        target = lax.rem(core + 1 + part // 2, 2)
        start = target * quarter + lax.rem(part, 2) * (width // 8)
        for step in range(width // 16):
            first = start + 2 * step
            rows = pl.ds(pl.multiple_of((half * count + first) * 8, 16), 16)
            words = table[rows, :].astype(F32)
            decoded = []
            for which in range(2):
                low = words[8 * which : 8 * which + 8, :128]
                high = words[8 * which : 8 * which + 8, 128:]
                code = index[pl.ds(first + which, 1), :]
                pieces = []
                for block in range(samples // 128):
                    picked = jnp.broadcast_to(code[:, block * 128 : block * 128 + 128], (8, 128))
                    place = picked & 127
                    a = jnp.take_along_axis(low, place, axis=1, mode="promise_in_bounds")
                    b = jnp.take_along_axis(high, place, axis=1, mode="promise_in_bounds")
                    pieces.append(jnp.where(picked < 128, a, b))
                decoded.append(jnp.concatenate(pieces, axis=1))
            rebuilt[part, step * 16 : step * 16 + 16, :] = jnp.concatenate(decoded, axis=0).astype(
                BF16
            )
        return carry

    lax.fori_loop(0, parts, decode, 0)
    for part in range(parts):
        out = (give, keep)[part // 2]
        start = (part % 2) * width
        out[:, start : start + width] = lax.dot_general(
            turned[...], rebuilt[part], NT, preferred_element_type=F32
        )


def covariance_part(where, features, codes, table):
    samples, rows = features.shape
    quarter = codes.shape[1] * 2
    out = jax.ShapeDtypeStruct((rows, quarter), F32)
    return call(
        covariance_kernel,
        [out, out],
        [where, features, codes, table],
        [
            pltpu.VMEM((rows, samples), BF16),
            pltpu.VMEM((codes.shape[1] // 2, samples), jnp.int32),
            pltpu.VMEM((4, quarter // 2, samples), BF16),
        ],
    )


OWN, Z1, Z2, Z3, Y2, Y1 = range(6)
WHOLE = 7
HALVES = ((OWN, Z2, 2), (OWN, Y2, 3), (Y2, Z2, 2))


def half_rows(where, u, v, side, rows):
    first = where[side] == 1
    left = jnp.where(first, u * rows, v * rows + rows // 2)
    right = jnp.where(first, v * rows, u * rows)
    return (
        pl.ds(pl.multiple_of(left, rows // 2), rows // 2),
        pl.ds(pl.multiple_of(right, rows), rows),
    )


def share(where, step, which):
    return lax.rem(where[1] + step, 4) * 2 + lax.rem(where[0] + which, 2)


def stack(high, low, refs):
    start = 0
    for ref in refs:
        place = slice(start, start + ref.shape[0])
        high[place, :], low[place, :] = split(ref[...])
        start += ref.shape[0]


def gram_kernel(where, own, z1, z3, y1, z2, y2, give, keep, high, low, gram):
    rows, depth = own.shape
    stack(high, low, (own, z1, z2, z3, y2, y1))
    column = sum(
        jnp.sum((ref[...] ** 2).reshape(rows // 8, 8, depth), axis=0) for ref in (own, z1, z2, z3)
    )
    squares = jnp.sum(column.reshape(8, -1, 128), axis=1)

    def pieces(first, last):
        return high[first * rows : last * rows, :], low[first * rows : last * rows, :]

    gram[:, : 2 * rows] = dot3(pieces(OWN, OWN + 1), pieces(OWN, Z1 + 1), NT)
    gram[:, 2 * rows : 6 * rows] = dot3(pieces(Y1, Y1 + 1), pieces(OWN, Z3 + 1), NT)
    gram[:, 6 * rows : 7 * rows] = dot3(pieces(Y2, Y2 + 1), pieces(Z1, Z1 + 1), NT)
    half, start = rows // 2, WHOLE * rows
    for u, v, side in HALVES:
        left, right = half_rows(where, u, v, side, rows)
        value = dot3((high[left, :], low[left, :]), (high[right, :], low[right, :]), NT)
        gram[:half, start : start + half] = value[:, :half]
        gram[half:, start : start + half] = value[:, half:]
        start += half
    piece, width = rows // 8, gram.shape[1]
    for step in range(4):
        for which, out in ((0, keep), (1, give)):
            place = share(where, step, which) * piece
            out[step, :, :width] = gram[pl.ds(pl.multiple_of(place, 8), piece), :]
            out[step, :8, width:] = squares
            out[step, 8:, width:] = jnp.zeros((piece - 8, 128), F32)


def gram_width(rows):
    return WHOLE * rows + len(HALVES) * rows // 2


def gram_part(where, own, near):
    rows, depth = own.shape
    width = gram_width(rows)
    out = jax.ShapeDtypeStruct((4, rows // 8, width + 128), F32)
    pair = jax.ShapeDtypeStruct((6 * rows, depth), BF16)
    return call(
        gram_kernel,
        [out, out, pair, pair],
        [where, own, *near],
        [pltpu.VMEM((rows, width), F32)],
        flops=6 * rows * width * depth,
    )


def collect(where, scale, shares, gram):
    factor = scale[0]
    factor = factor * factor
    for step in range(4):
        for which in range(2):
            value = shares[4 * which + step][:, : gram.shape[1]] * factor
            start = share(where, step, which) * value.shape[0]
            gram[pl.ds(pl.multiple_of(start, 8), value.shape[0]), :] = value


def along(gram, first, last):
    rows = gram.shape[0]
    return gram[:, first * rows : last * rows]


def across(gram, *blocks):
    turned = [along(gram, block, block + 1).T for block in blocks]
    return turned[0] if len(turned) == 1 else jnp.concatenate(turned, axis=1)


def times(left, high, low, first, last):
    rows = left.shape[0]
    place = slice(first * rows, last * rows)
    return dot3(split(left), (high[place, :], low[place, :]), NN)


def product_kernel(where, scale, *refs):
    shares, (high, low) = refs[:8], refs[8:10]
    to_z1, to_z3, to_y1, to_z2, to_y2, to_own, gram, sums = refs[10:]
    rows = to_own.shape[0]
    collect(where, scale, shares, gram)
    to_z1[...] = times(across(gram, 6, 3), high, low, Y2, Y1 + 1) + times(
        across(gram, 1), high, low, OWN, OWN + 1
    )
    to_z3[...] = times(across(gram, 5), high, low, Y1, Y1 + 1)
    to_y1[...] = times(along(gram, 2, 6), high, low, OWN, Z3 + 1)

    def sum_of(place):
        return sums.at[place * rows : place * rows + rows, :]

    sum_of(OWN)[...] = jnp.zeros(to_own.shape, F32)
    sum_of(Z2)[...] = times(across(gram, 4), high, low, Y1, Y1 + 1)
    sum_of(Y2)[...] = times(along(gram, 6, 7), high, low, Z1, Z1 + 1)
    half, start = rows // 2, WHOLE * rows
    for u, v, side in HALVES:
        left, right = half_rows(where, u, v, side, rows)
        folded = gram[:, start : start + half]
        value = jnp.concatenate([folded[:half, :], folded[half:, :]], axis=1)
        sums[left, :] += dot3(split(value), (high[right, :], low[right, :]), NN)
        sums[right, :] += dot3(split(value.T), (high[left, :], low[left, :]), NN)
        start += half
    to_z2[...] = sum_of(Z2)[...]
    to_y2[...] = sum_of(Y2)[...]
    to_own[...] = sum_of(OWN)[...]


def own_product_kernel(where, scale, *refs):
    shares, (high, low, part), (to_own, gram) = refs[:8], refs[8:11], refs[11:]
    collect(where, scale, shares, gram)
    to_own[...] = part[...] + (
        times(along(gram, 0, 2), high, low, OWN, Z1 + 1)
        + times(across(gram, 2), high, low, Y1, Y1 + 1)
    )


def product_part(kernel, count, blocks, where, scale, shares, pair, *more):
    rows, depth = pair[0].shape[0] // 6, pair[0].shape[1]
    width = 3 * rows if kernel is own_product_kernel else gram_width(rows)
    scratch = [pltpu.VMEM((rows, width), F32)]
    if kernel is product_kernel:
        scratch.append(pltpu.VMEM((5 * rows, depth), F32))
    return call(
        kernel,
        [jax.ShapeDtypeStruct((rows, depth), F32)] * count,
        [where, scale, *shares, *pair, *more],
        scratch,
        flops=6 * blocks * rows * rows * depth,
        n_scalars=2,
    )


def line(axis, shift):
    pairs = [(i, (i + shift) % 4) for i in range(4)]
    if axis == "x":
        spot = [0, 2, 1, 3]
        return ("xl", "xh"), [(spot[a], spot[b]) for a, b in pairs]
    return axis, pairs


def send(value, axis, shift):
    return lax.ppermute(value, *line(axis, shift))


def swap(value, axis):
    return lax.ppermute(value, axis, [(0, 1), (1, 0)])


def sum_over_x(give, keep):
    other = swap(give, "core")
    mine = keep[0] + other[0]
    for d in (2, 1, 3):
        mine = mine + send(keep[d] + other[d], "x", d)
    return mine


def on_device(features, codes, codebooks):
    core = lax.axis_index("core")
    xl = lax.axis_index("xl")
    x = lax.axis_index("xh") * 2 + xl
    sides = [lax.axis_index(axis) < 2 for axis in ("z", "y")]
    where = jnp.stack([core, x, *sides]).astype(jnp.int32)

    table = jnp.swapaxes(codebooks, 1, 2).reshape(-1, codebooks.shape[1])
    def half(which, features):
        chosen = jnp.concatenate([where, which[None].astype(jnp.int32)])
        return covariance_part(chosen, features, codes, table)

    give, keep = half(1 - xl, features)
    theirs, features = lax.optimization_barrier((keep + swap(give, "core"), features))
    theirs = swap(theirs, "xl")
    give, keep = half(xl, features)
    middle = give.shape[0] // 2
    from_core = [swap(piece, "core") for piece in (give[:middle], give[middle:])]
    current = (keep + jnp.concatenate(from_core, axis=0)) + theirs
    dimensions = features.shape[1] * 16
    moves = (("z", 1), ("z", -1), ("y", 1), ("z", 2), ("y", 2))

    for sweep in range(ITERS):
        near = [send(current, axis, -d) for axis, d in moves]
        give, keep, *pair = gram_part(where, current, near)
        mine = sum_over_x(give, keep)
        ours = [mine] + [send(mine, "x", -d) for d in (1, 2, 3)]
        if sweep == 0:
            squares = mine[:8, -128:]
            for bit in (1, 2):
                squares = squares + lax.ppermute(squares, "y", [(i, i ^ bit) for i in range(4)])
            ours[1], squares = lax.optimization_barrier((ours[1], squares))
            factor = start_scale * jnp.sqrt(dimensions / (jnp.sum(squares) + epsilon))
        else:
            factor = jnp.float32(1)
        shares = ours + [swap(piece, "core") for piece in ours]
        given = where, factor[None], shares, pair
        *pieces, part = product_part(product_kernel, 6, 13, *given)
        (value,) = product_part(own_product_kernel, 1, 3, *given, part)
        for piece, (axis, d) in zip(pieces, moves):
            value = value + send(piece, axis, d)
        current = factor * (1.5 * current - 0.5 * value)

    rank = xl * 2 + core
    rows = current.shape[0] // 4
    width = current.shape[1]
    out = jnp.zeros((rows, 4 * width), F32)
    for d in range(4):
        piece = lax.dynamic_slice_in_dim(current, (rank ^ d) * rows, rows, 0)
        if d:
            piece = lax.ppermute(piece, ("xl", "core"), [(i, i ^ d) for i in range(4)])
        out = lax.dynamic_update_slice_in_dim(out, piece, (rank ^ d) * width, 1)
    return out


def solution(mesh):
    devices = mesh.devices.reshape(2, 2, 4, 4, 2)
    return jax.shard_map(
        on_device,
        mesh=Mesh(devices, AXES),
        in_specs=(
            P(("xl", "core"), ("z", "y")),
            P(("xl", "core"), "xh"),
            P("xh", None, None),
        ),
        out_specs=P(("z", "y", "xl", "core"), "xh"),
        check_vma=False,
    )
```

```python
import functools

import jax
import jax.numpy as jnp
from jax import lax
from jax.experimental import pallas as pl
from jax.experimental.pallas import tpu as pltpu
from jax.sharding import Mesh, PartitionSpec as P

ITERS = 2

epsilon = 1e-06
start_scale = 0.45

F32 = jnp.float32
BF16 = jnp.bfloat16
AXES = ("xl", "core", "z", "y", "xh")
VMEM_BYTES = 20 * 1024 * 1024

NN = (((1,), (0,)), ((), ()))
NT = (((1,), (1,)), ((), ()))


def split(value):
    high = value.astype(BF16)
    return high, (value - high.astype(F32)).astype(BF16)


def dot3(a, b, dims):
    dot = functools.partial(lax.dot_general, dimension_numbers=dims, preferred_element_type=F32)
    return dot(a[0], b[0]) + (dot(a[0], b[1]) + dot(a[1], b[0]))


def call(kernel, out_shape, operands, scratch=(), flops=0, n_scalars=1):
    vmem = pl.BlockSpec(memory_space=pltpu.VMEM)
    smem = pl.BlockSpec(memory_space=pltpu.SMEM)
    moved = sum(o.size * o.dtype.itemsize for o in operands)
    moved += sum(o.size * o.dtype.itemsize for o in out_shape)
    return pl.pallas_call(
        kernel,
        out_shape=out_shape,
        in_specs=[smem] * n_scalars + [vmem] * (len(operands) - n_scalars),
        out_specs=[vmem] * len(out_shape),
        scratch_shapes=scratch,
        compiler_params=pltpu.CompilerParams(vmem_limit_bytes=VMEM_BYTES),
        cost_estimate=pl.CostEstimate(flops=flops, bytes_accessed=moved, transcendentals=0),
    )(*operands)


def covariance_kernel(where, features, codes, table, give, keep, turned, index, rebuilt):
    core, half = where[0], where[4]
    samples, count = codes.shape[0], index.shape[0]
    turned[...] = features[...].astype(F32).T.astype(BF16)
    index[...] = codes[:, pl.ds(pl.multiple_of(half * count, count), count)].T
    parts, width, _ = rebuilt.shape
    quarter = give.shape[1] // 8

    def decode(part, carry):
        target = lax.rem(core + 1 + part // 2, 2)
        start = target * quarter + lax.rem(part, 2) * (width // 8)
        for step in range(width // 16):
            first = start + 2 * step
            rows = pl.ds(pl.multiple_of((half * count + first) * 8, 16), 16)
            words = table[rows, :].astype(F32)
            decoded = []
            for which in range(2):
                low = words[8 * which : 8 * which + 8, :128]
                high = words[8 * which : 8 * which + 8, 128:]
                code = index[pl.ds(first + which, 1), :]
                pieces = []
                for block in range(samples // 128):
                    picked = jnp.broadcast_to(code[:, block * 128 : block * 128 + 128], (8, 128))
                    place = picked & 127
                    a = jnp.take_along_axis(low, place, axis=1, mode="promise_in_bounds")
                    b = jnp.take_along_axis(high, place, axis=1, mode="promise_in_bounds")
                    pieces.append(jnp.where(picked < 128, a, b))
                decoded.append(jnp.concatenate(pieces, axis=1))
            rebuilt[part, step * 16 : step * 16 + 16, :] = jnp.concatenate(decoded, axis=0).astype(
                BF16
            )
        return carry

    lax.fori_loop(0, parts, decode, 0)
    for part in range(parts):
        out = (give, keep)[part // 2]
        start = (part % 2) * width
        out[:, start : start + width] = lax.dot_general(
            turned[...], rebuilt[part], NT, preferred_element_type=F32
        )


def covariance_part(where, features, codes, table):
    samples, rows = features.shape
    quarter = codes.shape[1] * 2
    out = jax.ShapeDtypeStruct((rows, quarter), F32)
    return call(
        covariance_kernel,
        [out, out],
        [where, features, codes, table],
        [
            pltpu.VMEM((rows, samples), BF16),
            pltpu.VMEM((codes.shape[1] // 2, samples), jnp.int32),
            pltpu.VMEM((4, quarter // 2, samples), BF16),
        ],
    )


OWN, Z1, Z2, Z3, Y2, Y1 = range(6)
WHOLE = 7
HALVES = ((OWN, Z2, 2), (OWN, Y2, 3), (Y2, Z2, 2))


def half_rows(where, u, v, side, rows):
    first = where[side] == 1
    left = jnp.where(first, u * rows, v * rows + rows // 2)
    right = jnp.where(first, v * rows, u * rows)
    return (
        pl.ds(pl.multiple_of(left, rows // 2), rows // 2),
        pl.ds(pl.multiple_of(right, rows), rows),
    )


def share(where, step, which):
    return lax.rem(where[1] + step, 4) * 2 + lax.rem(where[0] + which, 2)


def stack(high, low, refs):
    start = 0
    for ref in refs:
        place = slice(start, start + ref.shape[0])
        high[place, :], low[place, :] = split(ref[...])
        start += ref.shape[0]


def gram_kernel(where, own, z1, z3, y1, z2, y2, give, keep, high, low, gram):
    rows, depth = own.shape
    stack(high, low, (own, z1, z2, z3, y2, y1))
    column = sum(
        jnp.sum((ref[...] ** 2).reshape(rows // 8, 8, depth), axis=0) for ref in (own, z1, z2, z3)
    )
    squares = jnp.sum(column.reshape(8, -1, 128), axis=1)

    def pieces(first, last):
        return high[first * rows : last * rows, :], low[first * rows : last * rows, :]

    gram[:, : 2 * rows] = dot3(pieces(OWN, OWN + 1), pieces(OWN, Z1 + 1), NT)
    gram[:, 2 * rows : 6 * rows] = dot3(pieces(Y1, Y1 + 1), pieces(OWN, Z3 + 1), NT)
    gram[:, 6 * rows : 7 * rows] = dot3(pieces(Y2, Y2 + 1), pieces(Z1, Z1 + 1), NT)
    half, start = rows // 2, WHOLE * rows
    for u, v, side in HALVES:
        left, right = half_rows(where, u, v, side, rows)
        value = dot3((high[left, :], low[left, :]), (high[right, :], low[right, :]), NT)
        gram[:half, start : start + half] = value[:, :half]
        gram[half:, start : start + half] = value[:, half:]
        start += half
    piece, width = rows // 8, gram.shape[1]
    for step in range(4):
        for which, out in ((0, keep), (1, give)):
            place = share(where, step, which) * piece
            out[step, :, :width] = gram[pl.ds(pl.multiple_of(place, 8), piece), :]
            out[step, :8, width:] = squares
            out[step, 8:, width:] = jnp.zeros((piece - 8, 128), F32)


def gram_width(rows):
    return WHOLE * rows + len(HALVES) * rows // 2


def gram_part(where, own, near):
    rows, depth = own.shape
    width = gram_width(rows)
    out = jax.ShapeDtypeStruct((4, rows // 8, width + 128), F32)
    pair = jax.ShapeDtypeStruct((6 * rows, depth), BF16)
    return call(
        gram_kernel,
        [out, out, pair, pair],
        [where, own, *near],
        [pltpu.VMEM((rows, width), F32)],
        flops=6 * rows * width * depth,
    )


def collect(where, scale, shares, gram):
    factor = scale[0]
    factor = factor * factor
    for step in range(4):
        for which in range(2):
            value = shares[4 * which + step][:, : gram.shape[1]] * factor
            start = share(where, step, which) * value.shape[0]
            gram[pl.ds(pl.multiple_of(start, 8), value.shape[0]), :] = value


def along(gram, first, last):
    rows = gram.shape[0]
    return gram[:, first * rows : last * rows]


def across(gram, *blocks):
    turned = [along(gram, block, block + 1).T for block in blocks]
    return turned[0] if len(turned) == 1 else jnp.concatenate(turned, axis=1)


def times(left, high, low, first, last):
    rows = left.shape[0]
    place = slice(first * rows, last * rows)
    return dot3(split(left), (high[place, :], low[place, :]), NN)


def near_product_kernel(where, scale, *refs):
    shares, (high, low), (to_z1, to_z3, to_y1, gram) = refs[:8], refs[8:10], refs[10:]
    collect(where, scale, shares, gram)
    to_z1[...] = times(across(gram, 6, 3), high, low, Y2, Y1 + 1) + times(
        across(gram, 1), high, low, OWN, OWN + 1
    )
    to_z3[...] = times(across(gram, 5), high, low, Y1, Y1 + 1)
    to_y1[...] = times(along(gram, 2, 6), high, low, OWN, Z3 + 1)


def far_product_kernel(where, gram, high, low, to_z2, to_y2, to_own, sums):
    rows = to_own.shape[0]

    def sum_of(place):
        return sums.at[place * rows : place * rows + rows, :]

    sum_of(OWN)[...] = jnp.zeros(to_own.shape, F32)
    sum_of(Z2)[...] = times(across(gram, 4), high, low, Y1, Y1 + 1)
    sum_of(Y2)[...] = times(along(gram, 6, 7), high, low, Z1, Z1 + 1)
    half, start = rows // 2, WHOLE * rows
    for u, v, side in HALVES:
        left, right = half_rows(where, u, v, side, rows)
        folded = gram[:, start : start + half]
        value = jnp.concatenate([folded[:half, :], folded[half:, :]], axis=1)
        sums[left, :] += dot3(split(value), (high[right, :], low[right, :]), NN)
        sums[right, :] += dot3(split(value.T), (high[left, :], low[left, :]), NN)
        start += half
    to_z2[...] = sum_of(Z2)[...]
    to_y2[...] = sum_of(Y2)[...]
    to_own[...] = sum_of(OWN)[...]


def own_product_kernel(where, gram, high, low, part, to_own):
    to_own[...] = part[...] + (
        times(along(gram, 0, 2), high, low, OWN, Z1 + 1)
        + times(across(gram, 2), high, low, Y1, Y1 + 1)
    )


def product_part(where, scale, shares, pair):
    rows, depth = pair[0].shape[0] // 6, pair[0].shape[1]
    out = jax.ShapeDtypeStruct((rows, depth), F32)
    blocks = jax.ShapeDtypeStruct((rows, gram_width(rows)), F32)
    flops = 6 * rows * rows * depth
    *near, gram = call(
        near_product_kernel,
        [out] * 3 + [blocks],
        [where, scale, *shares, *pair],
        flops=8 * flops,
        n_scalars=2,
    )
    *far, part = call(
        far_product_kernel,
        [out] * 3,
        [where, gram, *pair],
        [pltpu.VMEM((5 * rows, depth), F32)],
        flops=5 * flops,
    )
    own = call(own_product_kernel, [out], [where, gram, *pair, part], flops=3 * flops)
    return (*near, *far), own[0]


def line(axis, shift):
    pairs = [(i, (i + shift) % 4) for i in range(4)]
    if axis == "x":
        spot = [0, 2, 1, 3]
        return ("xl", "xh"), [(spot[a], spot[b]) for a, b in pairs]
    return axis, pairs


def send(value, axis, shift):
    return lax.ppermute(value, *line(axis, shift))


def swap(value, axis):
    return lax.ppermute(value, axis, [(0, 1), (1, 0)])


def sum_over_x(give, keep):
    other = swap(give, "core")
    mine = keep[0] + other[0]
    for d in (2, 1, 3):
        mine = mine + send(keep[d] + other[d], "x", d)
    return mine


def on_device(features, codes, codebooks):
    core = lax.axis_index("core")
    xl = lax.axis_index("xl")
    x = lax.axis_index("xh") * 2 + xl
    sides = [lax.axis_index(axis) < 2 for axis in ("z", "y")]
    where = jnp.stack([core, x, *sides]).astype(jnp.int32)

    table = jnp.swapaxes(codebooks, 1, 2).reshape(-1, codebooks.shape[1])
    def half(which, features):
        chosen = jnp.concatenate([where, which[None].astype(jnp.int32)])
        return covariance_part(chosen, features, codes, table)

    give, keep = half(1 - xl, features)
    theirs, features = lax.optimization_barrier((keep + swap(give, "core"), features))
    theirs = swap(theirs, "xl")
    give, keep = half(xl, features)
    middle = give.shape[0] // 2
    from_core = [swap(piece, "core") for piece in (give[:middle], give[middle:])]
    current = (keep + jnp.concatenate(from_core, axis=0)) + theirs
    dimensions = features.shape[1] * 16
    moves = (("z", 1), ("z", -1), ("y", 1), ("z", 2), ("y", 2))

    for sweep in range(ITERS):
        near = [send(current, axis, -d) for axis, d in moves]
        give, keep, *pair = gram_part(where, current, near)
        mine = sum_over_x(give, keep)
        ours = [mine] + [send(mine, "x", -d) for d in (1, 2, 3)]
        if sweep == 0:
            squares = mine[:8, -128:]
            for bit in (1, 2):
                squares = squares + lax.ppermute(squares, "y", [(i, i ^ bit) for i in range(4)])
            ours[1], squares = lax.optimization_barrier((ours[1], squares))
            factor = start_scale * jnp.sqrt(dimensions / (jnp.sum(squares) + epsilon))
        else:
            factor = jnp.float32(1)
        shares = ours + [swap(piece, "core") for piece in ours]
        pieces, value = product_part(where, factor[None], shares, pair)
        received = [send(piece, axis, d) for piece, (axis, d) in zip(pieces, moves)]
        value = value + received[0] + received[1] + received[2]
        value, *received = lax.optimization_barrier((value, received[3], received[4]))
        value = value + received[0] + received[1]
        current = factor * (1.5 * current - 0.5 * value)

    rank = xl * 2 + core
    rows = current.shape[0] // 4
    width = current.shape[1]
    out = jnp.zeros((rows, 4 * width), F32)
    for d in (0, 2, 3, 1):
        piece = lax.dynamic_slice_in_dim(current, (rank ^ d) * rows, rows, 0)
        if d:
            piece = lax.ppermute(piece, ("xl", "core"), [(i, i ^ d) for i in range(4)])
        out = lax.dynamic_update_slice_in_dim(out, piece, (rank ^ d) * width, 1)
    return out


def solution(mesh):
    devices = mesh.devices.reshape(2, 2, 4, 4, 2)
    return jax.shard_map(
        on_device,
        mesh=Mesh(devices, AXES),
        in_specs=(
            P(("xl", "core"), ("z", "y")),
            P(("xl", "core"), "xh"),
            P("xh", None, None),
        ),
        out_specs=P(("z", "y", "xl", "core"), "xh"),
        check_vma=False,
    )
```

```python
import functools

import jax
import jax.numpy as jnp
from jax import lax
from jax.experimental import pallas as pl
from jax.experimental.pallas import tpu as pltpu
from jax.sharding import Mesh, PartitionSpec as P

ITERS = 2

epsilon = 1e-06
start_scale = 0.45

F32 = jnp.float32
BF16 = jnp.bfloat16
AXES = ("xl", "core", "z", "y", "xh")
VMEM_BYTES = 20 * 1024 * 1024

NN = (((1,), (0,)), ((), ()))
NT = (((1,), (1,)), ((), ()))


def split(value):
    high = value.astype(BF16)
    return high, (value - high.astype(F32)).astype(BF16)


def dot3(a, b, dims):
    dot = functools.partial(lax.dot_general, dimension_numbers=dims, preferred_element_type=F32)
    return dot(a[0], b[0]) + (dot(a[0], b[1]) + dot(a[1], b[0]))


def call(kernel, out_shape, operands, scratch=(), flops=0, n_scalars=1):
    vmem = pl.BlockSpec(memory_space=pltpu.VMEM)
    smem = pl.BlockSpec(memory_space=pltpu.SMEM)
    moved = sum(o.size * o.dtype.itemsize for o in operands)
    moved += sum(o.size * o.dtype.itemsize for o in out_shape)
    return pl.pallas_call(
        kernel,
        out_shape=out_shape,
        in_specs=[smem] * n_scalars + [vmem] * (len(operands) - n_scalars),
        out_specs=[vmem] * len(out_shape),
        scratch_shapes=scratch,
        compiler_params=pltpu.CompilerParams(vmem_limit_bytes=VMEM_BYTES),
        cost_estimate=pl.CostEstimate(flops=flops, bytes_accessed=moved, transcendentals=0),
    )(*operands)


def covariance_kernel(where, features, codes, table, give, keep, turned, index, rebuilt):
    core, half = where[0], where[4]
    samples, count = codes.shape[0], index.shape[0]
    turned[...] = features[...].astype(F32).T.astype(BF16)
    index[...] = codes[:, pl.ds(pl.multiple_of(half * count, count), count)].T
    parts, width, _ = rebuilt.shape
    quarter = give.shape[1] // 8

    def decode(part, carry):
        target = lax.rem(core + 1 + part // 2, 2)
        start = target * quarter + lax.rem(part, 2) * (width // 8)
        for step in range(width // 16):
            first = start + 2 * step
            rows = pl.ds(pl.multiple_of((half * count + first) * 8, 16), 16)
            words = table[rows, :].astype(F32)
            decoded = []
            for which in range(2):
                low = words[8 * which : 8 * which + 8, :128]
                high = words[8 * which : 8 * which + 8, 128:]
                code = index[pl.ds(first + which, 1), :]
                pieces = []
                for block in range(samples // 128):
                    picked = jnp.broadcast_to(code[:, block * 128 : block * 128 + 128], (8, 128))
                    place = picked & 127
                    a = jnp.take_along_axis(low, place, axis=1, mode="promise_in_bounds")
                    b = jnp.take_along_axis(high, place, axis=1, mode="promise_in_bounds")
                    pieces.append(jnp.where(picked < 128, a, b))
                decoded.append(jnp.concatenate(pieces, axis=1))
            rebuilt[part, step * 16 : step * 16 + 16, :] = jnp.concatenate(decoded, axis=0).astype(
                BF16
            )
        return carry

    lax.fori_loop(0, parts, decode, 0)
    for part in range(parts):
        out = (give, keep)[part // 2]
        start = (part % 2) * width
        out[:, start : start + width] = lax.dot_general(
            turned[...], rebuilt[part], NT, preferred_element_type=F32
        )


def covariance_part(where, features, codes, table):
    samples, rows = features.shape
    quarter = codes.shape[1] * 2
    out = jax.ShapeDtypeStruct((rows, quarter), F32)
    return call(
        covariance_kernel,
        [out, out],
        [where, features, codes, table],
        [
            pltpu.VMEM((rows, samples), BF16),
            pltpu.VMEM((codes.shape[1] // 2, samples), jnp.int32),
            pltpu.VMEM((4, quarter // 2, samples), BF16),
        ],
    )


OWN, Z1, Z2, Z3, Y2, Y1 = range(6)
WHOLE = 7
HALVES = ((OWN, Z2, 2), (OWN, Y2, 3), (Y2, Z2, 2))


def half_rows(where, u, v, side, rows):
    first = where[side] == 1
    left = jnp.where(first, u * rows, v * rows + rows // 2)
    right = jnp.where(first, v * rows, u * rows)
    return (
        pl.ds(pl.multiple_of(left, rows // 2), rows // 2),
        pl.ds(pl.multiple_of(right, rows), rows),
    )


def share(where, step, which):
    return lax.rem(where[1] + step, 4) * 2 + lax.rem(where[0] + which, 2)


def gram_kernel(parts, where, *refs):
    order = OWN, Z1, Z3, Y1, Z2, Y2
    give, keep, high, low, gram = refs[6 * parts :]
    rows, depth = refs[0].shape[0] * parts, refs[0].shape[1]
    column = jnp.zeros((8, depth), F32)
    for number, ref in enumerate(refs[: 6 * parts]):
        piece = order[number % 6]
        start = piece * rows + number // 6 * (rows // parts)
        place = slice(start, start + rows // parts)
        value = ref[...]
        high[place, :], low[place, :] = split(value)
        if piece in (OWN, Z1, Z2, Z3):
            column = column + jnp.sum((value * value).reshape(-1, 8, depth), axis=0)
    squares = jnp.sum(column.reshape(8, -1, 128), axis=1)

    def pieces(first, last):
        return high[first * rows : last * rows, :], low[first * rows : last * rows, :]

    gram[:, : 2 * rows] = dot3(pieces(OWN, OWN + 1), pieces(OWN, Z1 + 1), NT)
    gram[:, 2 * rows : 6 * rows] = dot3(pieces(Y1, Y1 + 1), pieces(OWN, Z3 + 1), NT)
    gram[:, 6 * rows : 7 * rows] = dot3(pieces(Y2, Y2 + 1), pieces(Z1, Z1 + 1), NT)
    half, start = rows // 2, WHOLE * rows
    for u, v, side in HALVES:
        left, right = half_rows(where, u, v, side, rows)
        value = dot3((high[left, :], low[left, :]), (high[right, :], low[right, :]), NT)
        gram[:half, start : start + half] = value[:, :half]
        gram[half:, start : start + half] = value[:, half:]
        start += half
    piece, width = rows // 8, gram.shape[1]
    for step in range(4):
        for which, out in ((0, keep), (1, give)):
            place = share(where, step, which) * piece
            out[step, :, :width] = gram[pl.ds(pl.multiple_of(place, 8), piece), :]
            out[step, :8, width:] = squares
            out[step, 8:, width:] = jnp.zeros((piece - 8, 128), F32)


def gram_width(rows):
    return WHOLE * rows + len(HALVES) * rows // 2


def gram_part(where, pieces):
    parts = len(pieces)
    rows, depth = pieces[0][0].shape[0] * parts, pieces[0][0].shape[1]
    width = gram_width(rows)
    out = jax.ShapeDtypeStruct((4, rows // 8, width + 128), F32)
    pair = jax.ShapeDtypeStruct((6 * rows, depth), BF16)
    return call(
        functools.partial(gram_kernel, parts),
        [out, out, pair, pair],
        [where, *(piece for part in pieces for piece in part)],
        [pltpu.VMEM((rows, width), F32)],
        flops=6 * rows * width * depth,
    )


def collect(where, scale, shares, gram):
    factor = scale[0]
    factor = factor * factor
    for step in range(4):
        for which in range(2):
            value = shares[4 * which + step][:, : gram.shape[1]] * factor
            start = share(where, step, which) * value.shape[0]
            gram[pl.ds(pl.multiple_of(start, 8), value.shape[0]), :] = value


def along(gram, first, last):
    rows = gram.shape[0]
    return gram[:, first * rows : last * rows]


def across(gram, *blocks):
    turned = [along(gram, block, block + 1).T for block in blocks]
    return turned[0] if len(turned) == 1 else jnp.concatenate(turned, axis=1)


def times(left, high, low, first, last):
    rows = left.shape[0]
    place = slice(first * rows, last * rows)
    return dot3(split(left), (high[place, :], low[place, :]), NN)


def near_product_kernel(where, scale, *refs):
    shares, (high, low), (to_z1, to_z3, to_y1, gram) = refs[:8], refs[8:10], refs[10:]
    collect(where, scale, shares, gram)
    to_z1[...] = times(across(gram, 6, 3), high, low, Y2, Y1 + 1) + times(
        across(gram, 1), high, low, OWN, OWN + 1
    )
    to_z3[...] = times(across(gram, 5), high, low, Y1, Y1 + 1)
    to_y1[...] = times(along(gram, 2, 6), high, low, OWN, Z3 + 1)


def far_product_kernel(where, gram, high, low, to_z2, to_y2, to_own, sums):
    rows = to_own.shape[0]

    def sum_of(place):
        return sums.at[place * rows : place * rows + rows, :]

    sum_of(OWN)[...] = jnp.zeros(to_own.shape, F32)
    sum_of(Z2)[...] = times(across(gram, 4), high, low, Y1, Y1 + 1)
    sum_of(Y2)[...] = times(along(gram, 6, 7), high, low, Z1, Z1 + 1)
    half, start = rows // 2, WHOLE * rows
    for u, v, side in HALVES:
        left, right = half_rows(where, u, v, side, rows)
        folded = gram[:, start : start + half]
        value = jnp.concatenate([folded[:half, :], folded[half:, :]], axis=1)
        sums[left, :] += dot3(split(value), (high[right, :], low[right, :]), NN)
        sums[right, :] += dot3(split(value.T), (high[left, :], low[left, :]), NN)
        start += half
    to_z2[...] = sum_of(Z2)[...]
    to_y2[...] = sum_of(Y2)[...]
    to_own[...] = sum_of(OWN)[...]


def own_product_kernel(where, gram, high, low, part, to_own):
    to_own[...] = part[...] + (
        times(along(gram, 0, 2), high, low, OWN, Z1 + 1)
        + times(across(gram, 2), high, low, Y1, Y1 + 1)
    )


def product_part(where, scale, shares, pair):
    rows, depth = pair[0].shape[0] // 6, pair[0].shape[1]
    out = jax.ShapeDtypeStruct((rows, depth), F32)
    blocks = jax.ShapeDtypeStruct((rows, gram_width(rows)), F32)
    flops = 6 * rows * rows * depth
    *near, gram = call(
        near_product_kernel,
        [out] * 3 + [blocks],
        [where, scale, *shares, *pair],
        flops=8 * flops,
        n_scalars=2,
    )
    *far, part = call(
        far_product_kernel,
        [out] * 3,
        [where, gram, *pair],
        [pltpu.VMEM((5 * rows, depth), F32)],
        flops=5 * flops,
    )
    own = call(own_product_kernel, [out], [where, gram, *pair, part], flops=3 * flops)
    return (*near, *far), own[0]


def line(axis, shift):
    pairs = [(i, (i + shift) % 4) for i in range(4)]
    if axis == "x":
        spot = [0, 2, 1, 3]
        return ("xl", "xh"), [(spot[a], spot[b]) for a, b in pairs]
    return axis, pairs


def send(value, axis, shift):
    return lax.ppermute(value, *line(axis, shift))


def swap(value, axis):
    return lax.ppermute(value, axis, [(0, 1), (1, 0)])


def sum_over_x(give, keep):
    other = swap(give, "core")
    mine = keep[0] + other[0]
    for d in (2, 1, 3):
        mine = mine + send(keep[d] + other[d], "x", d)
    return mine


def after(value, *others):
    return lax.optimization_barrier((value, others))[0]


MOVES = (("z", 1), ("z", -1), ("y", 1), ("z", 2), ("y", 2))


def gather(part):
    return [part] + [send(part, axis, -d) for axis, d in MOVES]


def on_device(features, codes, codebooks):
    core = lax.axis_index("core")
    xl = lax.axis_index("xl")
    x = lax.axis_index("xh") * 2 + xl
    sides = [lax.axis_index(axis) < 2 for axis in ("z", "y")]
    where = jnp.stack([core, x, *sides]).astype(jnp.int32)

    table = jnp.swapaxes(codebooks, 1, 2).reshape(-1, codebooks.shape[1])
    def half(which, features):
        chosen = jnp.concatenate([where, which[None].astype(jnp.int32)])
        return covariance_part(chosen, features, codes, table)

    def halves(value):
        middle = value.shape[0] // 2
        return value[:middle], value[middle:]

    give, keep = half(1 - xl, features)
    theirs = halves(keep + swap(give, "core"))
    *theirs, features = lax.optimization_barrier((*theirs, features))
    first = swap(theirs[0], "xl")
    second = swap(after(theirs[1], first), "xl")
    give, keep = half(xl, features)
    upper, lower = halves(give)
    upper = jnp.concatenate([swap(piece, "core") for piece in halves(upper)], axis=0)
    lower = swap(lower, "core")
    keep = halves(keep)
    current = [upper + keep[0] + first]
    pieces = [gather(current[0])]
    current.append(lower + keep[1] + after(second, pieces[0][1]))
    pieces.append(gather(current[1]))
    dimensions = features.shape[1] * 16
    for sweep in range(ITERS):
        if sweep:
            pieces = [gather(current[0])]
        give, keep, *pair = gram_part(where, pieces)
        mine = sum_over_x(give, keep)
        ours = [mine] + [send(mine, "x", -d) for d in (1, 2, 3)]
        if sweep == 0:
            squares = mine[:8, -128:]
            for bit in (1, 2):
                squares = squares + lax.ppermute(squares, "y", [(i, i ^ bit) for i in range(4)])
            ours[1], squares = lax.optimization_barrier((ours[1], squares))
            factor = start_scale * jnp.sqrt(dimensions / (jnp.sum(squares) + epsilon))
        else:
            factor = jnp.float32(1)
        shares = ours + [swap(piece, "core") for piece in ours]
        pieces, value = product_part(where, factor[None], shares, pair)
        received = [send(piece, axis, d) for piece, (axis, d) in zip(pieces, MOVES)]
        value = value + received[0] + received[1] + received[2]
        value, *received = lax.optimization_barrier((value, received[3], received[4]))
        value = value + received[0] + received[1]
        current = [factor * (1.5 * jnp.concatenate(current, axis=0) - 0.5 * value)]

    current = current[0]
    rank = xl * 2 + core
    rows = current.shape[0] // 4
    width = current.shape[1]
    out = jnp.zeros((rows, 4 * width), F32)
    for d in (0, 2, 3, 1):
        piece = lax.dynamic_slice_in_dim(current, (rank ^ d) * rows, rows, 0)
        if d:
            piece = lax.ppermute(piece, ("xl", "core"), [(i, i ^ d) for i in range(4)])
        out = lax.dynamic_update_slice_in_dim(out, piece, (rank ^ d) * width, 1)
    return out


def solution(mesh):
    devices = mesh.devices.reshape(2, 2, 4, 4, 2)
    return jax.shard_map(
        on_device,
        mesh=Mesh(devices, AXES),
        in_specs=(
            P(("xl", "core"), ("z", "y")),
            P(("xl", "core"), "xh"),
            P("xh", None, None),
        ),
        out_specs=P(("z", "y", "xl", "core"), "xh"),
        check_vma=False,
    )
```

```python
import functools

import jax
import jax.numpy as jnp
from jax import lax
from jax.experimental import pallas as pl
from jax.experimental.pallas import tpu as pltpu
from jax.sharding import Mesh, PartitionSpec as P

ITERS = 2

epsilon = 1e-06
start_scale = 0.45

F32 = jnp.float32
BF16 = jnp.bfloat16
AXES = ("xl", "core", "z", "y", "xh")
VMEM_BYTES = 20 * 1024 * 1024

NN = (((1,), (0,)), ((), ()))
NT = (((1,), (1,)), ((), ()))


def split(value):
    high = value.astype(BF16)
    return high, (value - high.astype(F32)).astype(BF16)


def dot3(a, b, dims):
    dot = functools.partial(lax.dot_general, dimension_numbers=dims, preferred_element_type=F32)
    return dot(a[0], b[0]) + (dot(a[0], b[1]) + dot(a[1], b[0]))


def call(kernel, out_shape, operands, scratch=(), flops=0, n_scalars=1):
    vmem = pl.BlockSpec(memory_space=pltpu.VMEM)
    smem = pl.BlockSpec(memory_space=pltpu.SMEM)
    moved = sum(o.size * o.dtype.itemsize for o in operands)
    moved += sum(o.size * o.dtype.itemsize for o in out_shape)
    return pl.pallas_call(
        kernel,
        out_shape=out_shape,
        in_specs=[smem] * n_scalars + [vmem] * (len(operands) - n_scalars),
        out_specs=[vmem] * len(out_shape),
        scratch_shapes=scratch,
        compiler_params=pltpu.CompilerParams(vmem_limit_bytes=VMEM_BYTES),
        cost_estimate=pl.CostEstimate(flops=flops, bytes_accessed=moved, transcendentals=0),
    )(*operands)


def covariance_kernel(where, features, codes, table, give, keep, turned, index, rebuilt):
    core, half = where[0], where[4]
    samples, count = codes.shape[0], index.shape[0]
    turned[...] = features[...].astype(F32).T.astype(BF16)
    index[...] = codes[:, pl.ds(pl.multiple_of(half * count, count), count)].T
    parts, width, _ = rebuilt.shape
    quarter = give.shape[1] // 8

    def decode(place, carry):
        start = lax.rem(core + 1 + place, 2) * quarter
        for step in range(2 * width // 16):
            first = start + 2 * step
            rows = pl.ds(pl.multiple_of((half * count + first) * 8, 16), 16)
            words = table[rows, :].astype(F32)
            decoded = []
            for which in range(2):
                low = words[8 * which : 8 * which + 8, :128]
                high = words[8 * which : 8 * which + 8, 128:]
                code = index[pl.ds(first + which, 1), :]
                pieces = []
                for block in range(samples // 128):
                    picked = jnp.broadcast_to(code[:, block * 128 : block * 128 + 128], (8, 128))
                    entry = picked & 127
                    a = jnp.take_along_axis(low, entry, axis=1, mode="promise_in_bounds")
                    b = jnp.take_along_axis(high, entry, axis=1, mode="promise_in_bounds")
                    pieces.append(jnp.where(picked < 128, a, b))
                decoded.append(jnp.concatenate(pieces, axis=1))
            row = step * 16 % width
            rebuilt[2 * place + step * 16 // width, row : row + 16, :] = jnp.concatenate(
                decoded, axis=0
            ).astype(BF16)
        return carry

    lax.fori_loop(0, 2, decode, 0)
    for part in range(parts):
        out = (give, keep)[part // 2]
        start = (part % 2) * width
        out[:, start : start + width] = lax.dot_general(
            turned[...], rebuilt[part], NT, preferred_element_type=F32
        )


def covariance_part(where, features, codes, table):
    samples, rows = features.shape
    quarter = codes.shape[1] * 2
    out = jax.ShapeDtypeStruct((rows, quarter), F32)
    return call(
        covariance_kernel,
        [out, out],
        [where, features, codes, table],
        [
            pltpu.VMEM((rows, samples), BF16),
            pltpu.VMEM((codes.shape[1] // 2, samples), jnp.int32),
            pltpu.VMEM((4, quarter // 2, samples), BF16),
        ],
    )


OWN, Z1, Z2, Z3, Y2, Y1 = range(6)
WHOLE = 7
STEPS = (0, 2, 1, 3)
HALVES = ((OWN, Z2, 2), (OWN, Y2, 3), (Y2, Z2, 2))


def half_rows(where, u, v, side, rows):
    first = where[side] == 1
    left = jnp.where(first, u * rows, v * rows + rows // 2)
    right = jnp.where(first, v * rows, u * rows)
    return (
        pl.ds(pl.multiple_of(left, rows // 2), rows // 2),
        pl.ds(pl.multiple_of(right, rows), rows),
    )


def share(where, step, which):
    return lax.rem(where[1] + step, 4) * 2 + lax.rem(where[0] + which, 2)


def stack(high, low, refs):
    start = 0
    for ref in refs:
        place = slice(start, start + ref.shape[0])
        high[place, :], low[place, :] = split(ref[...])
        start += ref.shape[0]


def gram_kernel(where, own, z1, z3, y1, z2, y2, give, keep, high, low, gram):
    rows, depth = own.shape
    stack(high, low, (own, z1, z2, z3, y2, y1))
    column = sum(
        jnp.sum((ref[...] ** 2).reshape(rows // 8, 8, depth), axis=0) for ref in (own, z1, z2, z3)
    )
    squares = jnp.sum(column.reshape(8, -1, 128), axis=1)

    def pieces(first, last):
        return high[first * rows : last * rows, :], low[first * rows : last * rows, :]

    gram[:, : 2 * rows] = dot3(pieces(OWN, OWN + 1), pieces(OWN, Z1 + 1), NT)
    gram[:, 2 * rows : 6 * rows] = dot3(pieces(Y1, Y1 + 1), pieces(OWN, Z3 + 1), NT)
    gram[:, 6 * rows : 7 * rows] = dot3(pieces(Y2, Y2 + 1), pieces(Z1, Z1 + 1), NT)
    half, start = rows // 2, WHOLE * rows
    for u, v, side in HALVES:
        left, right = half_rows(where, u, v, side, rows)
        value = dot3((high[left, :], low[left, :]), (high[right, :], low[right, :]), NT)
        gram[:half, start : start + half] = value[:, :half]
        gram[half:, start : start + half] = value[:, half:]
        start += half
    piece, width = rows // 8, gram.shape[1]
    for step in range(4):
        for which, out in ((0, keep), (1, give)):
            place = share(where, step, which) * piece
            out[step, :, :width] = gram[pl.ds(pl.multiple_of(place, 8), piece), :]
            out[step, :8, width:] = squares
            out[step, 8:, width:] = jnp.zeros((piece - 8, 128), F32)


def gram_width(rows):
    return WHOLE * rows + len(HALVES) * rows // 2


def gram_part(where, own, near):
    rows, depth = own.shape
    width = gram_width(rows)
    out = jax.ShapeDtypeStruct((4, rows // 8, width + 128), F32)
    pair = jax.ShapeDtypeStruct((6 * rows, depth), BF16)
    return call(
        gram_kernel,
        [out, out, pair, pair],
        [where, own, *near],
        [pltpu.VMEM((rows, width), F32)],
        flops=6 * rows * width * depth,
    )


def collect(where, scale, shares, gram):
    factor = scale[0]
    factor = factor * factor
    for number, step in enumerate(STEPS):
        for which in range(2):
            value = shares[4 * which + number][:, : gram.shape[1]] * factor
            start = share(where, step, which) * value.shape[0]
            gram[pl.ds(pl.multiple_of(start, 8), value.shape[0]), :] = value


def along(gram, first, last):
    rows = gram.shape[0]
    return gram[:, first * rows : last * rows]


def across(gram, *blocks):
    turned = [along(gram, block, block + 1).T for block in blocks]
    return turned[0] if len(turned) == 1 else jnp.concatenate(turned, axis=1)


def times(left, high, low, first, last):
    rows = left.shape[0]
    place = slice(first * rows, last * rows)
    return dot3(split(left), (high[place, :], low[place, :]), NN)


def near_product_kernel(where, scale, *refs):
    shares, (high, low), (to_z1, to_z3, to_y1, gram) = refs[:8], refs[8:10], refs[10:]
    collect(where, scale, shares, gram)
    to_z1[...] = times(across(gram, 6, 3), high, low, Y2, Y1 + 1) + times(
        across(gram, 1), high, low, OWN, OWN + 1
    )
    to_z3[...] = times(across(gram, 5), high, low, Y1, Y1 + 1)
    to_y1[...] = times(along(gram, 2, 6), high, low, OWN, Z3 + 1)


def far_product_kernel(where, gram, high, low, to_z2, to_y2, to_own, sums):
    rows = to_own.shape[0]

    def sum_of(place):
        return sums.at[place * rows : place * rows + rows, :]

    sum_of(OWN)[...] = jnp.zeros(to_own.shape, F32)
    sum_of(Z2)[...] = times(across(gram, 4), high, low, Y1, Y1 + 1)
    sum_of(Y2)[...] = times(along(gram, 6, 7), high, low, Z1, Z1 + 1)
    half, start = rows // 2, WHOLE * rows
    for u, v, side in HALVES:
        left, right = half_rows(where, u, v, side, rows)
        folded = gram[:, start : start + half]
        value = jnp.concatenate([folded[:half, :], folded[half:, :]], axis=1)
        sums[left, :] += dot3(split(value), (high[right, :], low[right, :]), NN)
        sums[right, :] += dot3(split(value.T), (high[left, :], low[left, :]), NN)
        start += half
    to_z2[...] = sum_of(Z2)[...]
    to_y2[...] = sum_of(Y2)[...]
    to_own[...] = sum_of(OWN)[...]


def own_product_kernel(where, gram, high, low, part, to_own):
    to_own[...] = part[...] + (
        times(along(gram, 0, 2), high, low, OWN, Z1 + 1)
        + times(across(gram, 2), high, low, Y1, Y1 + 1)
    )


def product_part(where, scale, shares, pair):
    rows, depth = pair[0].shape[0] // 6, pair[0].shape[1]
    out = jax.ShapeDtypeStruct((rows, depth), F32)
    blocks = jax.ShapeDtypeStruct((rows, gram_width(rows)), F32)
    flops = 6 * rows * rows * depth
    *near, gram = call(
        near_product_kernel,
        [out] * 3 + [blocks],
        [where, scale, *shares, *pair],
        flops=8 * flops,
        n_scalars=2,
    )
    *far, part = call(
        far_product_kernel,
        [out] * 3,
        [where, gram, *pair],
        [pltpu.VMEM((5 * rows, depth), F32)],
        flops=5 * flops,
    )
    own = call(own_product_kernel, [out], [where, gram, *pair, part], flops=3 * flops)
    return (*near, *far), own[0]


def line(axis, shift):
    pairs = [(i, (i + shift) % 4) for i in range(4)]
    if axis == "x":
        spot = [0, 2, 1, 3]
        return ("xl", "xh"), [(spot[a], spot[b]) for a, b in pairs]
    return axis, pairs


def send(value, axis, shift):
    return lax.ppermute(value, *line(axis, shift))


def swap(value, axis):
    return lax.ppermute(value, axis, [(0, 1), (1, 0)])


def sum_over_x(give, keep):
    other = swap(give, "core")
    mine = keep[0] + other[0]
    for d in (2, 1, 3):
        mine = mine + send(keep[d] + other[d], "x", d)
    return mine


def on_device(features, codes, codebooks):
    core = lax.axis_index("core")
    xl = lax.axis_index("xl")
    x = lax.axis_index("xh") * 2 + xl
    sides = [lax.axis_index(axis) < 2 for axis in ("z", "y")]
    where = jnp.stack([core, x, *sides]).astype(jnp.int32)

    table = jnp.swapaxes(codebooks, 1, 2).reshape(-1, codebooks.shape[1])
    def half(which, features):
        chosen = jnp.concatenate([where, which[None].astype(jnp.int32)])
        return covariance_part(chosen, features, codes, table)

    give, keep = half(1 - xl, features)
    theirs, features = lax.optimization_barrier((keep + swap(give, "core"), features))
    theirs = swap(theirs, "xl")
    give, keep = half(xl, features)
    middle = give.shape[0] // 2
    from_core = [swap(piece, "core") for piece in (give[:middle], give[middle:])]
    ours = lax.optimization_barrier(keep + jnp.concatenate(from_core, axis=0))
    current = ours + theirs
    dimensions = features.shape[1] * 16
    moves = (("z", 1), ("z", -1), ("y", 1), ("z", 2), ("y", 2))

    for sweep in range(ITERS):
        near = [send(current, axis, -d) for axis, d in moves]
        give, keep, *pair = gram_part(where, current, near)
        mine = sum_over_x(give, keep)
        ours = [mine] + [send(mine, "x", -d) for d in STEPS[1:]]
        if sweep == 0:
            squares = mine[:8, -128:]
            for bit in (1, 2):
                squares = squares + lax.ppermute(squares, "y", [(i, i ^ bit) for i in range(4)])
            ours[1], squares = lax.optimization_barrier((ours[1], squares))
            factor = start_scale * jnp.sqrt(dimensions / (jnp.sum(squares) + epsilon))
        else:
            factor = jnp.float32(1)
        shares = ours + [swap(piece, "core") for piece in ours]
        pieces, value = product_part(where, factor[None], shares, pair)
        received = [send(piece, axis, d) for piece, (axis, d) in zip(pieces, moves)]
        value = value + received[0] + received[1] + received[2]
        value, *received = lax.optimization_barrier((value, received[3], received[4]))
        value = value + received[0] + received[1]
        current = factor * (1.5 * current - 0.5 * value)

    rank = xl * 2 + core
    rows = current.shape[0] // 4
    width = current.shape[1]
    out = jnp.zeros((rows, 4 * width), F32)
    for d in (0, 2, 3, 1):
        piece = lax.dynamic_slice_in_dim(current, (rank ^ d) * rows, rows, 0)
        if d:
            piece = lax.ppermute(piece, ("xl", "core"), [(i, i ^ d) for i in range(4)])
        out = lax.dynamic_update_slice_in_dim(out, piece, (rank ^ d) * width, 1)
    return out


def solution(mesh):
    devices = mesh.devices.reshape(2, 2, 4, 4, 2)
    return jax.shard_map(
        on_device,
        mesh=Mesh(devices, AXES),
        in_specs=(
            P(("xl", "core"), ("z", "y")),
            P(("xl", "core"), "xh"),
            P("xh", None, None),
        ),
        out_specs=P(("z", "y", "xl", "core"), "xh"),
        check_vma=False,
    )
```

```python
import functools

import jax
import jax.numpy as jnp
from jax import lax
from jax.experimental import pallas as pl
from jax.experimental.pallas import tpu as pltpu
from jax.sharding import Mesh, PartitionSpec as P

ITERS = 2

epsilon = 1e-06
start_scale = 0.45

F32 = jnp.float32
BF16 = jnp.bfloat16
AXES = ("xl", "core", "z", "y", "xh")
VMEM_BYTES = 20 * 1024 * 1024
FETCH_BYTES = 56 * 1024 * 1024

NN = (((1,), (0,)), ((), ()))
NT = (((1,), (1,)), ((), ()))


def split(value):
    high = value.astype(BF16)
    return high, (value - high.astype(F32)).astype(BF16)


def dot3(a, b, dims):
    dot = functools.partial(lax.dot_general, dimension_numbers=dims, preferred_element_type=F32)
    return dot(a[0], b[0]) + (dot(a[0], b[1]) + dot(a[1], b[0]))


def call(kernel, out_shape, operands, scratch=(), flops=0, n_scalars=1, space=pltpu.VMEM, limit=VMEM_BYTES):
    vmem = pl.BlockSpec(memory_space=pltpu.VMEM)
    smem = pl.BlockSpec(memory_space=pltpu.SMEM)
    moved = sum(o.size * o.dtype.itemsize for o in operands)
    moved += sum(o.size * o.dtype.itemsize for o in out_shape)
    return pl.pallas_call(
        kernel,
        out_shape=out_shape,
        in_specs=[smem] * n_scalars
        + [pl.BlockSpec(memory_space=space)] * (len(operands) - n_scalars),
        out_specs=[vmem] * len(out_shape),
        scratch_shapes=scratch,
        compiler_params=pltpu.CompilerParams(vmem_limit_bytes=limit),
        cost_estimate=pl.CostEstimate(flops=flops, bytes_accessed=moved, transcendentals=0),
    )(*operands)


def covariance_kernel(where, all_features, all_codes, all_words, give, keep, *scratch):
    features, codes, table, done, turned, index, rebuilt = scratch
    core, half = where[0], where[4]
    samples, count = codes.shape
    chosen = pl.ds(pl.multiple_of(half * count, count), count)
    words = pl.ds(pl.multiple_of(half * count * 8, count * 8), count * 8)
    fetch = [
        pltpu.make_async_copy(all_codes.at[:, chosen], codes, done.at[0]),
        pltpu.make_async_copy(all_words.at[words, :], table, done.at[1]),
        pltpu.make_async_copy(all_features, features, done.at[2]),
    ]
    for copy in fetch:
        copy.start()
    fetch[0].wait()
    index[...] = codes[...].T
    fetch[1].wait()
    parts, width, _ = rebuilt.shape
    quarter = give.shape[1] // 8

    def decode(place, carry):
        start = lax.rem(core + 1 + place, 2) * quarter
        for step in range(2 * width // 16):
            first = start + 2 * step
            rows = pl.ds(pl.multiple_of(first * 8, 16), 16)
            words = table[rows, :].astype(F32)
            decoded = []
            for which in range(2):
                low = words[8 * which : 8 * which + 8, :128]
                high = words[8 * which : 8 * which + 8, 128:]
                code = index[pl.ds(first + which, 1), :]
                pieces = []
                for block in range(samples // 128):
                    picked = jnp.broadcast_to(code[:, block * 128 : block * 128 + 128], (8, 128))
                    entry = picked & 127
                    a = jnp.take_along_axis(low, entry, axis=1, mode="promise_in_bounds")
                    b = jnp.take_along_axis(high, entry, axis=1, mode="promise_in_bounds")
                    pieces.append(jnp.where(picked < 128, a, b))
                decoded.append(jnp.concatenate(pieces, axis=1))
            row = step * 16 % width
            rebuilt[2 * place + step * 16 // width, row : row + 16, :] = jnp.concatenate(
                decoded, axis=0
            ).astype(BF16)
        return carry

    lax.fori_loop(0, 2, decode, 0)
    fetch[2].wait()
    turned[...] = features[...].astype(F32).T.astype(BF16)
    for part in range(parts):
        out = (give, keep)[part // 2]
        start = (part % 2) * width
        out[:, start : start + width] = lax.dot_general(
            turned[...], rebuilt[part], NT, preferred_element_type=F32
        )


def covariance_part(where, features, codes, table, limit):
    samples, rows = features.shape
    quarter = codes.shape[1] * 2
    out = jax.ShapeDtypeStruct((rows, quarter), F32)
    return call(
        covariance_kernel,
        [out, out],
        [where, features, codes, table],
        [
            pltpu.VMEM((samples, rows), BF16),
            pltpu.VMEM((samples, codes.shape[1] // 2), jnp.int32),
            pltpu.VMEM((table.shape[0] // 2, table.shape[1]), BF16),
            pltpu.SemaphoreType.DMA((3,)),
            pltpu.VMEM((rows, samples), BF16),
            pltpu.VMEM((codes.shape[1] // 2, samples), jnp.int32),
            pltpu.VMEM((4, quarter // 2, samples), BF16),
        ],
        space=pltpu.HBM,
        limit=limit,
    )


OWN, Z1, Z2, Z3, Y2, Y1 = range(6)
WHOLE = 7
STEPS = (0, 2, 1, 3)
HALVES = ((OWN, Z2, 2), (OWN, Y2, 3), (Y2, Z2, 2))


def half_rows(where, u, v, side, rows):
    first = where[side] == 1
    left = jnp.where(first, u * rows, v * rows + rows // 2)
    right = jnp.where(first, v * rows, u * rows)
    return (
        pl.ds(pl.multiple_of(left, rows // 2), rows // 2),
        pl.ds(pl.multiple_of(right, rows), rows),
    )


def share(where, step, which):
    return lax.rem(where[1] + step, 4) * 2 + lax.rem(where[0] + which, 2)


def stack(high, low, refs):
    start = 0
    for ref in refs:
        place = slice(start, start + ref.shape[0])
        high[place, :], low[place, :] = split(ref[...])
        start += ref.shape[0]


def gram_kernel(where, own, z1, z3, y1, z2, y2, give, keep, high, low, gram):
    rows, depth = own.shape
    stack(high, low, (own, z1, z2, z3, y2, y1))
    column = sum(
        jnp.sum((ref[...] ** 2).reshape(rows // 8, 8, depth), axis=0) for ref in (own, z1, z2, z3)
    )
    squares = jnp.sum(column.reshape(8, -1, 128), axis=1)

    def pieces(first, last):
        return high[first * rows : last * rows, :], low[first * rows : last * rows, :]

    gram[:, : 2 * rows] = dot3(pieces(OWN, OWN + 1), pieces(OWN, Z1 + 1), NT)
    gram[:, 2 * rows : 6 * rows] = dot3(pieces(Y1, Y1 + 1), pieces(OWN, Z3 + 1), NT)
    gram[:, 6 * rows : 7 * rows] = dot3(pieces(Y2, Y2 + 1), pieces(Z1, Z1 + 1), NT)
    half, start = rows // 2, WHOLE * rows
    for u, v, side in HALVES:
        left, right = half_rows(where, u, v, side, rows)
        value = dot3((high[left, :], low[left, :]), (high[right, :], low[right, :]), NT)
        gram[:half, start : start + half] = value[:, :half]
        gram[half:, start : start + half] = value[:, half:]
        start += half
    piece, width = rows // 8, gram.shape[1]
    for step in range(4):
        for which, out in ((0, keep), (1, give)):
            place = share(where, step, which) * piece
            out[step, :, :width] = gram[pl.ds(pl.multiple_of(place, 8), piece), :]
            out[step, :8, width:] = squares
            out[step, 8:, width:] = jnp.zeros((piece - 8, 128), F32)


def gram_width(rows):
    return WHOLE * rows + len(HALVES) * rows // 2


def gram_part(where, own, near):
    rows, depth = own.shape
    width = gram_width(rows)
    out = jax.ShapeDtypeStruct((4, rows // 8, width + 128), F32)
    pair = jax.ShapeDtypeStruct((6 * rows, depth), BF16)
    return call(
        gram_kernel,
        [out, out, pair, pair],
        [where, own, *near],
        [pltpu.VMEM((rows, width), F32)],
        flops=6 * rows * width * depth,
    )


def collect(where, scale, shares, gram):
    factor = scale[0]
    factor = factor * factor
    for number, step in enumerate(STEPS):
        for which in range(2):
            value = shares[4 * which + number][:, : gram.shape[1]] * factor
            start = share(where, step, which) * value.shape[0]
            gram[pl.ds(pl.multiple_of(start, 8), value.shape[0]), :] = value


def along(gram, first, last):
    rows = gram.shape[0]
    return gram[:, first * rows : last * rows]


def across(gram, *blocks):
    turned = [along(gram, block, block + 1).T for block in blocks]
    return turned[0] if len(turned) == 1 else jnp.concatenate(turned, axis=1)


def times(left, high, low, first, last):
    rows = left.shape[0]
    place = slice(first * rows, last * rows)
    return dot3(split(left), (high[place, :], low[place, :]), NN)


def near_product_kernel(where, scale, *refs):
    shares, (high, low), (to_z1, to_z3, to_y1, gram) = refs[:8], refs[8:10], refs[10:]
    collect(where, scale, shares, gram)
    to_z1[...] = times(across(gram, 6, 3), high, low, Y2, Y1 + 1) + times(
        across(gram, 1), high, low, OWN, OWN + 1
    )
    to_z3[...] = times(across(gram, 5), high, low, Y1, Y1 + 1)
    to_y1[...] = times(along(gram, 2, 6), high, low, OWN, Z3 + 1)


def far_product_kernel(where, gram, high, low, to_z2, to_y2, to_own, sums):
    rows = to_own.shape[0]

    def sum_of(place):
        return sums.at[place * rows : place * rows + rows, :]

    sum_of(OWN)[...] = jnp.zeros(to_own.shape, F32)
    sum_of(Z2)[...] = times(across(gram, 4), high, low, Y1, Y1 + 1)
    sum_of(Y2)[...] = times(along(gram, 6, 7), high, low, Z1, Z1 + 1)
    half, start = rows // 2, WHOLE * rows
    for u, v, side in HALVES:
        left, right = half_rows(where, u, v, side, rows)
        folded = gram[:, start : start + half]
        value = jnp.concatenate([folded[:half, :], folded[half:, :]], axis=1)
        sums[left, :] += dot3(split(value), (high[right, :], low[right, :]), NN)
        sums[right, :] += dot3(split(value.T), (high[left, :], low[left, :]), NN)
        start += half
    to_z2[...] = sum_of(Z2)[...]
    to_y2[...] = sum_of(Y2)[...]
    to_own[...] = sum_of(OWN)[...]


def own_product_kernel(where, gram, high, low, part, to_own):
    to_own[...] = part[...] + (
        times(along(gram, 0, 2), high, low, OWN, Z1 + 1)
        + times(across(gram, 2), high, low, Y1, Y1 + 1)
    )


def product_part(where, scale, shares, pair):
    rows, depth = pair[0].shape[0] // 6, pair[0].shape[1]
    out = jax.ShapeDtypeStruct((rows, depth), F32)
    blocks = jax.ShapeDtypeStruct((rows, gram_width(rows)), F32)
    flops = 6 * rows * rows * depth
    *near, gram = call(
        near_product_kernel,
        [out] * 3 + [blocks],
        [where, scale, *shares, *pair],
        flops=8 * flops,
        n_scalars=2,
    )
    *far, part = call(
        far_product_kernel,
        [out] * 3,
        [where, gram, *pair],
        [pltpu.VMEM((5 * rows, depth), F32)],
        flops=5 * flops,
    )
    own = call(own_product_kernel, [out], [where, gram, *pair, part], flops=3 * flops)
    return (*near, *far), own[0]


def line(axis, shift):
    pairs = [(i, (i + shift) % 4) for i in range(4)]
    if axis == "x":
        spot = [0, 2, 1, 3]
        return ("xl", "xh"), [(spot[a], spot[b]) for a, b in pairs]
    return axis, pairs


def send(value, axis, shift):
    return lax.ppermute(value, *line(axis, shift))


def swap(value, axis):
    return lax.ppermute(value, axis, [(0, 1), (1, 0)])


def sum_over_x(give, keep):
    other = swap(give, "core")
    mine = keep[0] + other[0]
    for d in (2, 1, 3):
        mine = mine + send(keep[d] + other[d], "x", d)
    return mine


def on_device(features, codes, codebooks):
    core = lax.axis_index("core")
    xl = lax.axis_index("xl")
    x = lax.axis_index("xh") * 2 + xl
    sides = [lax.axis_index(axis) < 2 for axis in ("z", "y")]
    where = jnp.stack([core, x, *sides]).astype(jnp.int32)

    table = jnp.swapaxes(codebooks, 1, 2).reshape(-1, codebooks.shape[1])
    def half(which, features, limit):
        chosen = jnp.concatenate([where, which[None].astype(jnp.int32)])
        return covariance_part(chosen, features, codes, table, limit)

    give, keep = half(1 - xl, features, FETCH_BYTES)
    theirs, features = lax.optimization_barrier((keep + swap(give, "core"), features))
    theirs = swap(theirs, "xl")
    give, keep = half(xl, features, VMEM_BYTES)
    middle = give.shape[0] // 2
    from_core = [swap(piece, "core") for piece in (give[:middle], give[middle:])]
    ours = lax.optimization_barrier(keep + jnp.concatenate(from_core, axis=0))
    current = ours + theirs
    dimensions = features.shape[1] * 16
    moves = (("z", 1), ("z", -1), ("y", 1), ("z", 2), ("y", 2))

    for sweep in range(ITERS):
        near = [send(current, axis, -d) for axis, d in moves]
        give, keep, *pair = gram_part(where, current, near)
        mine = sum_over_x(give, keep)
        ours = [mine] + [send(mine, "x", -d) for d in STEPS[1:]]
        if sweep == 0:
            squares = mine[:8, -128:]
            for bit in (1, 2):
                squares = squares + lax.ppermute(squares, "y", [(i, i ^ bit) for i in range(4)])
            ours[1], squares = lax.optimization_barrier((ours[1], squares))
            factor = start_scale * jnp.sqrt(dimensions / (jnp.sum(squares) + epsilon))
        else:
            factor = jnp.float32(1)
        shares = ours + [swap(piece, "core") for piece in ours]
        pieces, value = product_part(where, factor[None], shares, pair)
        received = [send(piece, axis, d) for piece, (axis, d) in zip(pieces, moves)]
        value = value + received[0] + received[1] + received[2]
        value, *received = lax.optimization_barrier((value, received[3], received[4]))
        value = value + received[0] + received[1]
        current = factor * (1.5 * current - 0.5 * value)

    rank = xl * 2 + core
    rows = current.shape[0] // 4
    width = current.shape[1]
    out = jnp.zeros((rows, 4 * width), F32)
    for d in (0, 2, 3, 1):
        piece = lax.dynamic_slice_in_dim(current, (rank ^ d) * rows, rows, 0)
        if d:
            piece = lax.ppermute(piece, ("xl", "core"), [(i, i ^ d) for i in range(4)])
        out = lax.dynamic_update_slice_in_dim(out, piece, (rank ^ d) * width, 1)
    return out


def solution(mesh):
    devices = mesh.devices.reshape(2, 2, 4, 4, 2)
    return jax.shard_map(
        on_device,
        mesh=Mesh(devices, AXES),
        in_specs=(
            P(("xl", "core"), ("z", "y")),
            P(("xl", "core"), "xh"),
            P("xh", None, None),
        ),
        out_specs=P(("z", "y", "xl", "core"), "xh"),
        check_vma=False,
    )
```

```python
import functools

import jax
import jax.numpy as jnp
from jax import lax
from jax.experimental import pallas as pl
from jax.experimental.pallas import tpu as pltpu
from jax.sharding import Mesh, PartitionSpec as P

ITERS = 2

epsilon = 1e-06
start_scale = 0.45

F32 = jnp.float32
BF16 = jnp.bfloat16
AXES = ("xl", "core", "z", "y", "xh")
VMEM_BYTES = 16 * 1024 * 1024
FETCH_BYTES = 56 * 1024 * 1024

NN = (((1,), (0,)), ((), ()))
NT = (((1,), (1,)), ((), ()))


def split(value):
    high = value.astype(BF16)
    return high, (value - high.astype(F32)).astype(BF16)


def dot3(a, b, dims):
    dot = functools.partial(lax.dot_general, dimension_numbers=dims, preferred_element_type=F32)
    return dot(a[0], b[0]) + (dot(a[0], b[1]) + dot(a[1], b[0]))


def call(kernel, out_shape, operands, scratch=(), flops=0, n_scalars=1, space=pltpu.VMEM, limit=VMEM_BYTES):
    vmem = pl.BlockSpec(memory_space=pltpu.VMEM)
    smem = pl.BlockSpec(memory_space=pltpu.SMEM)
    moved = sum(o.size * o.dtype.itemsize for o in operands)
    moved += sum(o.size * o.dtype.itemsize for o in out_shape)
    return pl.pallas_call(
        kernel,
        out_shape=out_shape,
        in_specs=[smem] * n_scalars
        + [pl.BlockSpec(memory_space=space)] * (len(operands) - n_scalars),
        out_specs=[vmem] * len(out_shape),
        scratch_shapes=scratch,
        compiler_params=pltpu.CompilerParams(vmem_limit_bytes=limit),
        cost_estimate=pl.CostEstimate(flops=flops, bytes_accessed=moved, transcendentals=0),
    )(*operands)


def covariance_kernel(where, all_features, all_codes, all_words, give, keep, *scratch):
    features, codes, table, done, turned, index, rebuilt = scratch
    core, half = where[0], where[4]
    samples, count = codes.shape
    chosen = pl.ds(pl.multiple_of(half * count, count), count)
    words = pl.ds(pl.multiple_of(half * count * 8, count * 8), count * 8)
    fetch = [
        pltpu.make_async_copy(all_codes.at[:, chosen], codes, done.at[0]),
        pltpu.make_async_copy(all_words.at[words, :], table, done.at[1]),
        pltpu.make_async_copy(all_features, features, done.at[2]),
    ]
    for copy in fetch:
        copy.start()
    fetch[0].wait()
    index[...] = codes[...].T
    fetch[1].wait()
    parts, width, _ = rebuilt.shape
    quarter = give.shape[1] // 8

    def decode(place, carry):
        start = lax.rem(core + 1 + place, 2) * quarter
        for step in range(2 * width // 16):
            first = start + 2 * step
            rows = pl.ds(pl.multiple_of(first * 8, 16), 16)
            words = table[rows, :].astype(F32)
            decoded = []
            for which in range(2):
                low = words[8 * which : 8 * which + 8, :128]
                high = words[8 * which : 8 * which + 8, 128:]
                code = index[pl.ds(first + which, 1), :]
                pieces = []
                for block in range(samples // 128):
                    picked = jnp.broadcast_to(code[:, block * 128 : block * 128 + 128], (8, 128))
                    entry = picked & 127
                    a = jnp.take_along_axis(low, entry, axis=1, mode="promise_in_bounds")
                    b = jnp.take_along_axis(high, entry, axis=1, mode="promise_in_bounds")
                    pieces.append(jnp.where(picked < 128, a, b))
                decoded.append(jnp.concatenate(pieces, axis=1))
            row = step * 16 % width
            rebuilt[2 * place + step * 16 // width, row : row + 16, :] = jnp.concatenate(
                decoded, axis=0
            ).astype(BF16)
        return carry

    lax.fori_loop(0, 2, decode, 0)
    fetch[2].wait()
    turned[...] = features[...].astype(F32).T.astype(BF16)
    for part in range(parts):
        out = (give, keep)[part // 2]
        start = (part % 2) * width
        out[:, start : start + width] = lax.dot_general(
            turned[...], rebuilt[part], NT, preferred_element_type=F32
        )


def covariance_part(where, features, codes, table, limit):
    samples, rows = features.shape
    quarter = codes.shape[1] * 2
    out = jax.ShapeDtypeStruct((rows, quarter), F32)
    return call(
        covariance_kernel,
        [out, out],
        [where, features, codes, table],
        [
            pltpu.VMEM((samples, rows), BF16),
            pltpu.VMEM((samples, codes.shape[1] // 2), jnp.int32),
            pltpu.VMEM((table.shape[0] // 2, table.shape[1]), BF16),
            pltpu.SemaphoreType.DMA((3,)),
            pltpu.VMEM((rows, samples), BF16),
            pltpu.VMEM((codes.shape[1] // 2, samples), jnp.int32),
            pltpu.VMEM((4, quarter // 2, samples), BF16),
        ],
        space=pltpu.HBM,
        limit=limit,
    )


OWN, Z1, Z2, Z3, Y2, Y1 = range(6)
WHOLE = 7
STEPS = (0, 2, 1, 3)
HALVES = ((OWN, Z2, 2), (OWN, Y2, 3), (Y2, Z2, 2))


def half_rows(where, u, v, side, rows):
    first = where[side] == 1
    left = jnp.where(first, u * rows, v * rows + rows // 2)
    right = jnp.where(first, v * rows, u * rows)
    return (
        pl.ds(pl.multiple_of(left, rows // 2), rows // 2),
        pl.ds(pl.multiple_of(right, rows), rows),
    )


def share(where, step, which):
    return lax.rem(where[1] + step, 4) * 2 + lax.rem(where[0] + which, 2)


def stack(high, low, refs):
    start = 0
    for ref in refs:
        place = slice(start, start + ref.shape[0])
        high[place, :], low[place, :] = split(ref[...])
        start += ref.shape[0]


def gram_kernel(where, own, z1, z3, y1, z2, y2, give, keep, high, low, gram):
    rows, depth = own.shape
    stack(high, low, (own, z1, z2, z3, y2, y1))
    column = sum(
        jnp.sum((ref[...] ** 2).reshape(rows // 8, 8, depth), axis=0) for ref in (own, z1, z2, z3)
    )
    squares = jnp.sum(column.reshape(8, -1, 128), axis=1)

    def pieces(first, last):
        return high[first * rows : last * rows, :], low[first * rows : last * rows, :]

    gram[:, : 2 * rows] = dot3(pieces(OWN, OWN + 1), pieces(OWN, Z1 + 1), NT)
    gram[:, 2 * rows : 6 * rows] = dot3(pieces(Y1, Y1 + 1), pieces(OWN, Z3 + 1), NT)
    gram[:, 6 * rows : 7 * rows] = dot3(pieces(Y2, Y2 + 1), pieces(Z1, Z1 + 1), NT)
    half, start = rows // 2, WHOLE * rows
    for u, v, side in HALVES:
        left, right = half_rows(where, u, v, side, rows)
        value = dot3((high[left, :], low[left, :]), (high[right, :], low[right, :]), NT)
        gram[:half, start : start + half] = value[:, :half]
        gram[half:, start : start + half] = value[:, half:]
        start += half
    piece, width = rows // 8, gram.shape[1]
    for step in range(4):
        for which, out in ((0, keep), (1, give)):
            place = share(where, step, which) * piece
            out[step, :, :width] = gram[pl.ds(pl.multiple_of(place, 8), piece), :]
            out[step, :8, width:] = squares
            out[step, 8:, width:] = jnp.zeros((piece - 8, 128), F32)


def gram_width(rows):
    return WHOLE * rows + len(HALVES) * rows // 2


def gram_part(where, own, near):
    rows, depth = own.shape
    width = gram_width(rows)
    out = jax.ShapeDtypeStruct((4, rows // 8, width + 128), F32)
    pair = jax.ShapeDtypeStruct((6 * rows, depth), BF16)
    return call(
        gram_kernel,
        [out, out, pair, pair],
        [where, own, *near],
        [pltpu.VMEM((rows, width), F32)],
        flops=6 * rows * width * depth,
    )


def collect(where, scale, shares, gram):
    factor = scale[0]
    factor = factor * factor
    for number, step in enumerate(STEPS):
        for which in range(2):
            value = shares[4 * which + number][:, : gram.shape[1]] * factor
            start = share(where, step, which) * value.shape[0]
            gram[pl.ds(pl.multiple_of(start, 8), value.shape[0]), :] = value


def along(gram, first, last):
    rows = gram.shape[0]
    return gram[:, first * rows : last * rows]


def across(gram, *blocks):
    turned = [along(gram, block, block + 1).T for block in blocks]
    return turned[0] if len(turned) == 1 else jnp.concatenate(turned, axis=1)


def times(left, high, low, first, last):
    rows = left.shape[0]
    place = slice(first * rows, last * rows)
    return dot3(split(left), (high[place, :], low[place, :]), NN)


def near_product_kernel(where, scale, *refs):
    shares, (high, low), (to_z1, to_z3, to_y1, gram) = refs[:8], refs[8:10], refs[10:]
    collect(where, scale, shares, gram)
    to_z1[...] = times(across(gram, 6, 3), high, low, Y2, Y1 + 1) + times(
        across(gram, 1), high, low, OWN, OWN + 1
    )
    to_z3[...] = times(across(gram, 5), high, low, Y1, Y1 + 1)
    to_y1[...] = times(along(gram, 2, 6), high, low, OWN, Z3 + 1)


def far_product_kernel(where, gram, high, low, to_z2, to_y2, to_own, sums):
    rows = to_own.shape[0]

    def sum_of(place):
        return sums.at[place * rows : place * rows + rows, :]

    sum_of(OWN)[...] = jnp.zeros(to_own.shape, F32)
    sum_of(Z2)[...] = times(across(gram, 4), high, low, Y1, Y1 + 1)
    sum_of(Y2)[...] = times(along(gram, 6, 7), high, low, Z1, Z1 + 1)
    half, start = rows // 2, WHOLE * rows
    for u, v, side in HALVES:
        left, right = half_rows(where, u, v, side, rows)
        folded = gram[:, start : start + half]
        value = jnp.concatenate([folded[:half, :], folded[half:, :]], axis=1)
        sums[left, :] += dot3(split(value), (high[right, :], low[right, :]), NN)
        sums[right, :] += dot3(split(value.T), (high[left, :], low[left, :]), NN)
        start += half
    to_z2[...] = sum_of(Z2)[...]
    to_y2[...] = sum_of(Y2)[...]
    to_own[...] = sum_of(OWN)[...]


def own_product_kernel(where, gram, high, low, part, to_own):
    to_own[...] = part[...] + (
        times(along(gram, 0, 2), high, low, OWN, Z1 + 1)
        + times(across(gram, 2), high, low, Y1, Y1 + 1)
    )


def product_part(where, scale, shares, pair):
    rows, depth = pair[0].shape[0] // 6, pair[0].shape[1]
    out = jax.ShapeDtypeStruct((rows, depth), F32)
    blocks = jax.ShapeDtypeStruct((rows, gram_width(rows)), F32)
    flops = 6 * rows * rows * depth
    *near, gram = call(
        near_product_kernel,
        [out] * 3 + [blocks],
        [where, scale, *shares, *pair],
        flops=8 * flops,
        n_scalars=2,
    )
    *far, part = call(
        far_product_kernel,
        [out] * 3,
        [where, gram, *pair],
        [pltpu.VMEM((5 * rows, depth), F32)],
        flops=5 * flops,
    )
    own = call(own_product_kernel, [out], [where, gram, *pair, part], flops=3 * flops)
    return (*near, *far), own[0]


PARTNERS = (0, 2, 3, 1)


def spot(where, partner):
    return (lax.rem(where[1], 2) * 2 + where[0]) ^ partner


def update_kernel(where, current, value, *refs):
    addends, outs = refs[:2], refs[2:]
    rows = outs[0].shape[0]
    for partner, out in zip(PARTNERS, outs):
        place = pl.ds(pl.multiple_of(spot(where, partner) * rows, rows), rows)
        total = value[place, :] + addends[0][place, :] + addends[1][place, :]
        out[...] = 1.5 * current[place, :] - 0.5 * total


def join_kernel(where, *refs):
    pieces, out = refs[:-1], refs[-1]
    width = pieces[0].shape[1]
    for partner, piece in zip(PARTNERS, pieces):
        place = pl.ds(pl.multiple_of(spot(where, partner) * width, width), width)
        out[:, place] = piece[...]


def line(axis, shift):
    pairs = [(i, (i + shift) % 4) for i in range(4)]
    if axis == "x":
        spot = [0, 2, 1, 3]
        return ("xl", "xh"), [(spot[a], spot[b]) for a, b in pairs]
    return axis, pairs


def send(value, axis, shift):
    return lax.ppermute(value, *line(axis, shift))


def swap(value, axis):
    return lax.ppermute(value, axis, [(0, 1), (1, 0)])


def sum_over_x(give, keep):
    other = swap(give, "core")
    mine = keep[0] + other[0]
    for d in (2, 1, 3):
        mine = mine + send(keep[d] + other[d], "x", d)
    return mine


def on_device(features, codes, codebooks):
    core = lax.axis_index("core")
    xl = lax.axis_index("xl")
    x = lax.axis_index("xh") * 2 + xl
    sides = [lax.axis_index(axis) < 2 for axis in ("z", "y")]
    where = jnp.stack([core, x, *sides]).astype(jnp.int32)

    table = jnp.swapaxes(codebooks, 1, 2).reshape(-1, codebooks.shape[1])
    def half(which, features, limit):
        chosen = jnp.concatenate([where, which[None].astype(jnp.int32)])
        return covariance_part(chosen, features, codes, table, limit)

    give, keep = half(1 - xl, features, FETCH_BYTES)
    theirs, features = lax.optimization_barrier((keep + swap(give, "core"), features))
    theirs = swap(theirs, "xl")
    give, keep = half(xl, features, VMEM_BYTES)
    middle = give.shape[0] // 2
    from_core = [swap(piece, "core") for piece in (give[:middle], give[middle:])]
    ours = lax.optimization_barrier(keep + jnp.concatenate(from_core, axis=0))
    current = ours + theirs
    dimensions = features.shape[1] * 16
    moves = (("z", 1), ("z", -1), ("y", 1), ("z", 2), ("y", 2))

    for sweep in range(ITERS):
        near = [send(current, axis, -d) for axis, d in moves]
        give, keep, *pair = gram_part(where, current, near)
        mine = sum_over_x(give, keep)
        ours = [mine] + [send(mine, "x", -d) for d in STEPS[1:]]
        if sweep == 0:
            squares = mine[:8, -128:]
            for bit in (1, 2):
                squares = squares + lax.ppermute(squares, "y", [(i, i ^ bit) for i in range(4)])
            ours[1], squares = lax.optimization_barrier((ours[1], squares))
            factor = start_scale * jnp.sqrt(dimensions / (jnp.sum(squares) + epsilon))
        else:
            factor = jnp.float32(1)
        shares = ours + [swap(piece, "core") for piece in ours]
        pieces, value = product_part(where, factor[None], shares, pair)
        received = [send(piece, axis, d) for piece, (axis, d) in zip(pieces, moves)]
        value = value + received[0] + received[1] + received[2]
        value, *received = lax.optimization_barrier((value, received[3], received[4]))
        if sweep < ITERS - 1:
            current = factor * (1.5 * current - 0.5 * (value + received[0] + received[1]))

    rows, width = current.shape
    piece = jax.ShapeDtypeStruct((rows // 4, width), F32)
    pieces = list(call(update_kernel, [piece] * 4, [where, current, value, *received]))
    for number, partner in enumerate(PARTNERS):
        if partner:
            pairs = [(i, i ^ partner) for i in range(4)]
            pieces[number] = lax.ppermute(pieces[number], ("xl", "core"), pairs)
    whole = jax.ShapeDtypeStruct((rows // 4, 4 * width), F32)
    return call(join_kernel, [whole], [where, *pieces])[0]


def solution(mesh):
    devices = mesh.devices.reshape(2, 2, 4, 4, 2)
    return jax.shard_map(
        on_device,
        mesh=Mesh(devices, AXES),
        in_specs=(
            P(("xl", "core"), ("z", "y")),
            P(("xl", "core"), "xh"),
            P("xh", None, None),
        ),
        out_specs=P(("z", "y", "xl", "core"), "xh"),
        check_vma=False,
    )
```

```python
import functools

import jax
import jax.numpy as jnp
from jax import lax
from jax.experimental import pallas as pl
from jax.experimental.pallas import tpu as pltpu
from jax.sharding import Mesh, PartitionSpec as P

ITERS = 2

epsilon = 1e-06
start_scale = 0.45

F32 = jnp.float32
BF16 = jnp.bfloat16
AXES = ("xl", "core", "z", "y", "xh")
VMEM_BYTES = 16 * 1024 * 1024
FETCH_BYTES = 51 * 1024 * 1024

NN = (((1,), (0,)), ((), ()))
NT = (((1,), (1,)), ((), ()))


def split(value):
    high = value.astype(BF16)
    return high, (value - high.astype(F32)).astype(BF16)


def dot3(a, b, dims):
    dot = functools.partial(lax.dot_general, dimension_numbers=dims, preferred_element_type=F32)
    return dot(a[0], b[0]) + (dot(a[0], b[1]) + dot(a[1], b[0]))


def call(kernel, out_shape, operands, scratch=(), flops=0, n_scalars=1, space=pltpu.VMEM, limit=VMEM_BYTES):
    vmem = pl.BlockSpec(memory_space=pltpu.VMEM)
    smem = pl.BlockSpec(memory_space=pltpu.SMEM)
    moved = sum(o.size * o.dtype.itemsize for o in operands)
    moved += sum(o.size * o.dtype.itemsize for o in out_shape)
    return pl.pallas_call(
        kernel,
        out_shape=out_shape,
        in_specs=[smem] * n_scalars
        + [pl.BlockSpec(memory_space=space)] * (len(operands) - n_scalars),
        out_specs=[vmem] * len(out_shape),
        scratch_shapes=scratch,
        compiler_params=pltpu.CompilerParams(vmem_limit_bytes=limit),
        cost_estimate=pl.CostEstimate(flops=flops, bytes_accessed=moved, transcendentals=0),
    )(*operands)


def covariance_kernel(where, all_features, all_codes, all_words, give, keep, *scratch):
    features, codes, table, done, turned, index, rebuilt = scratch
    core, half = where[0], where[4]
    samples, count = codes.shape
    chosen = pl.ds(pl.multiple_of(half * count, count), count)
    words = pl.ds(pl.multiple_of(half * count * 8, count * 8), count * 8)
    fetch = [
        pltpu.make_async_copy(all_codes.at[:, chosen], codes, done.at[0]),
        pltpu.make_async_copy(all_words.at[words, :], table, done.at[1]),
        pltpu.make_async_copy(all_features, features, done.at[2]),
    ]
    for copy in fetch:
        copy.start()
    fetch[0].wait()
    index[...] = codes[...].T
    fetch[1].wait()
    parts, width, _ = rebuilt.shape
    quarter = give.shape[1] // 8

    def decode(place, carry):
        start = lax.rem(core + 1 + place, 2) * quarter
        for step in range(2 * width // 16):
            first = start + 2 * step
            rows = pl.ds(pl.multiple_of(first * 8, 16), 16)
            words = table[rows, :].astype(F32)
            decoded = []
            for which in range(2):
                low = words[8 * which : 8 * which + 8, :128]
                high = words[8 * which : 8 * which + 8, 128:]
                code = index[pl.ds(first + which, 1), :]
                pieces = []
                for block in range(samples // 128):
                    picked = jnp.broadcast_to(code[:, block * 128 : block * 128 + 128], (8, 128))
                    entry = picked & 127
                    a = jnp.take_along_axis(low, entry, axis=1, mode="promise_in_bounds")
                    b = jnp.take_along_axis(high, entry, axis=1, mode="promise_in_bounds")
                    pieces.append(jnp.where(picked < 128, a, b))
                decoded.append(jnp.concatenate(pieces, axis=1))
            row = step * 16 % width
            rebuilt[2 * place + step * 16 // width, row : row + 16, :] = jnp.concatenate(
                decoded, axis=0
            ).astype(BF16)
        return carry

    lax.fori_loop(0, 2, decode, 0)
    fetch[2].wait()
    turned[...] = features[...].astype(F32).T.astype(BF16)
    for part in range(parts):
        out = (give, keep)[part // 2]
        start = (part % 2) * width
        out[:, start : start + width] = lax.dot_general(
            turned[...], rebuilt[part], NT, preferred_element_type=F32
        )


def covariance_part(where, features, codes, table, limit):
    samples, rows = features.shape
    quarter = codes.shape[1] * 2
    out = jax.ShapeDtypeStruct((rows, quarter), F32)
    return call(
        covariance_kernel,
        [out, out],
        [where, features, codes, table],
        [
            pltpu.VMEM((samples, rows), BF16),
            pltpu.VMEM((samples, codes.shape[1] // 2), jnp.int32),
            pltpu.VMEM((table.shape[0] // 2, table.shape[1]), BF16),
            pltpu.SemaphoreType.DMA((3,)),
            pltpu.VMEM((rows, samples), BF16),
            pltpu.VMEM((codes.shape[1] // 2, samples), jnp.int32),
            pltpu.VMEM((4, quarter // 2, samples), BF16),
        ],
        space=pltpu.HBM,
        limit=limit,
    )


OWN, Z1, Z2, Z3, Y2, Y1 = range(6)
WHOLE = 7
STEPS = (0, 2, 1, 3)
HALVES = ((OWN, Z2, 2), (OWN, Y2, 3), (Y2, Z2, 2))


def half_rows(where, u, v, side, rows):
    first = where[side] == 1
    left = jnp.where(first, u * rows, v * rows + rows // 2)
    right = jnp.where(first, v * rows, u * rows)
    return (
        pl.ds(pl.multiple_of(left, rows // 2), rows // 2),
        pl.ds(pl.multiple_of(right, rows), rows),
    )


def share(where, step, which):
    return lax.rem(where[1] + step, 4) * 2 + lax.rem(where[0] + which, 2)


def stack(high, low, refs):
    start = 0
    for ref in refs:
        place = slice(start, start + ref.shape[0])
        high[place, :], low[place, :] = split(ref[...])
        start += ref.shape[0]


def gram_kernel(where, own, y2, z2, y1, z3, z1, give, keep, high, low, gram):
    rows, depth = own.shape
    stack(high, low, (own, z1, z2, z3, y2, y1))
    column = sum(
        jnp.sum((ref[...] ** 2).reshape(rows // 8, 8, depth), axis=0) for ref in (own, z1, z2, z3)
    )
    squares = jnp.sum(column.reshape(8, -1, 128), axis=1)

    def pieces(first, last):
        return high[first * rows : last * rows, :], low[first * rows : last * rows, :]

    gram[:, : 2 * rows] = dot3(pieces(OWN, OWN + 1), pieces(OWN, Z1 + 1), NT)
    gram[:, 2 * rows : 6 * rows] = dot3(pieces(Y1, Y1 + 1), pieces(OWN, Z3 + 1), NT)
    gram[:, 6 * rows : 7 * rows] = dot3(pieces(Y2, Y2 + 1), pieces(Z1, Z1 + 1), NT)
    half, start = rows // 2, WHOLE * rows
    for u, v, side in HALVES:
        left, right = half_rows(where, u, v, side, rows)
        value = dot3((high[left, :], low[left, :]), (high[right, :], low[right, :]), NT)
        gram[:half, start : start + half] = value[:, :half]
        gram[half:, start : start + half] = value[:, half:]
        start += half
    piece, width = rows // 8, gram.shape[1]
    for step in range(4):
        for which, out in ((0, keep), (1, give)):
            place = share(where, step, which) * piece
            out[step, :, :width] = gram[pl.ds(pl.multiple_of(place, 8), piece), :]
            out[step, :8, width:] = squares
            out[step, 8:, width:] = jnp.zeros((piece - 8, 128), F32)


def gram_width(rows):
    return WHOLE * rows + len(HALVES) * rows // 2


def gram_part(where, own, near):
    rows, depth = own.shape
    width = gram_width(rows)
    out = jax.ShapeDtypeStruct((4, rows // 8, width + 128), F32)
    pair = jax.ShapeDtypeStruct((6 * rows, depth), BF16)
    return call(
        gram_kernel,
        [out, out, pair, pair],
        [where, own, *near],
        [pltpu.VMEM((rows, width), F32)],
        flops=6 * rows * width * depth,
    )


def collect(where, scale, shares, gram):
    factor = scale[0]
    factor = factor * factor
    for number, step in enumerate(STEPS):
        for which in range(2):
            value = shares[4 * which + number][:, : gram.shape[1]] * factor
            start = share(where, step, which) * value.shape[0]
            gram[pl.ds(pl.multiple_of(start, 8), value.shape[0]), :] = value


def along(gram, first, last):
    rows = gram.shape[0]
    return gram[:, first * rows : last * rows]


def across(gram, *blocks):
    turned = [along(gram, block, block + 1).T for block in blocks]
    return turned[0] if len(turned) == 1 else jnp.concatenate(turned, axis=1)


def times(left, high, low, first, last):
    rows = left.shape[0]
    place = slice(first * rows, last * rows)
    return dot3(split(left), (high[place, :], low[place, :]), NN)


def near_product_kernel(where, scale, *refs):
    shares, (high, low), (to_z1, to_z3, to_y1, gram) = refs[:8], refs[8:10], refs[10:]
    collect(where, scale, shares, gram)
    to_z1[...] = times(across(gram, 6, 3), high, low, Y2, Y1 + 1) + times(
        across(gram, 1), high, low, OWN, OWN + 1
    )
    to_z3[...] = times(across(gram, 5), high, low, Y1, Y1 + 1)
    to_y1[...] = times(along(gram, 2, 6), high, low, OWN, Z3 + 1)


def far_product_kernel(where, gram, high, low, to_z2, to_y2, to_own, sums):
    rows = to_own.shape[0]

    def sum_of(place):
        return sums.at[place * rows : place * rows + rows, :]

    sum_of(OWN)[...] = jnp.zeros(to_own.shape, F32)
    sum_of(Z2)[...] = times(across(gram, 4), high, low, Y1, Y1 + 1)
    sum_of(Y2)[...] = times(along(gram, 6, 7), high, low, Z1, Z1 + 1)
    half, start = rows // 2, WHOLE * rows
    for u, v, side in HALVES:
        left, right = half_rows(where, u, v, side, rows)
        folded = gram[:, start : start + half]
        value = jnp.concatenate([folded[:half, :], folded[half:, :]], axis=1)
        sums[left, :] += dot3(split(value), (high[right, :], low[right, :]), NN)
        sums[right, :] += dot3(split(value.T), (high[left, :], low[left, :]), NN)
        start += half
    to_z2[...] = sum_of(Z2)[...]
    to_y2[...] = sum_of(Y2)[...]
    to_own[...] = sum_of(OWN)[...]


def own_product_kernel(where, gram, high, low, part, to_own):
    to_own[...] = part[...] + (
        times(along(gram, 0, 2), high, low, OWN, Z1 + 1)
        + times(across(gram, 2), high, low, Y1, Y1 + 1)
    )


def product_part(where, scale, shares, pair):
    rows, depth = pair[0].shape[0] // 6, pair[0].shape[1]
    out = jax.ShapeDtypeStruct((rows, depth), F32)
    blocks = jax.ShapeDtypeStruct((rows, gram_width(rows)), F32)
    flops = 6 * rows * rows * depth
    *near, gram = call(
        near_product_kernel,
        [out] * 3 + [blocks],
        [where, scale, *shares, *pair],
        flops=8 * flops,
        n_scalars=2,
    )
    *far, part = call(
        far_product_kernel,
        [out] * 3,
        [where, gram, *pair],
        [pltpu.VMEM((5 * rows, depth), F32)],
        flops=5 * flops,
    )
    own = call(own_product_kernel, [out], [where, gram, *pair, part], flops=3 * flops)
    return (*near, *far), own[0]


PARTNERS = (0, 2, 3, 1)


def spot(where, partner):
    return (lax.rem(where[1], 2) * 2 + where[0]) ^ partner


def update_kernel(where, current, value, *refs):
    addends, outs = refs[:2], refs[2:]
    rows = outs[0].shape[0]
    for partner, out in zip(PARTNERS, outs):
        place = pl.ds(pl.multiple_of(spot(where, partner) * rows, rows), rows)
        total = value[place, :] + addends[0][place, :] + addends[1][place, :]
        out[...] = 1.5 * current[place, :] - 0.5 * total


def join_kernel(where, *refs):
    pieces, out = refs[:-1], refs[-1]
    width = pieces[0].shape[1]
    for partner, piece in zip(PARTNERS, pieces):
        place = pl.ds(pl.multiple_of(spot(where, partner) * width, width), width)
        out[:, place] = piece[...]


def line(axis, shift):
    pairs = [(i, (i + shift) % 4) for i in range(4)]
    if axis == "x":
        spot = [0, 2, 1, 3]
        return ("xl", "xh"), [(spot[a], spot[b]) for a, b in pairs]
    return axis, pairs


def send(value, axis, shift):
    return lax.ppermute(value, *line(axis, shift))


def swap(value, axis):
    return lax.ppermute(value, axis, [(0, 1), (1, 0)])


def sum_over_x(give, keep):
    other = swap(give, "core")
    mine = keep[0] + other[0]
    for d in (2, 1, 3):
        mine = mine + send(keep[d] + other[d], "x", d)
    return mine


def on_device(features, codes, codebooks):
    core = lax.axis_index("core")
    xl = lax.axis_index("xl")
    x = lax.axis_index("xh") * 2 + xl
    sides = [lax.axis_index(axis) < 2 for axis in ("z", "y")]
    where = jnp.stack([core, x, *sides]).astype(jnp.int32)

    table = jnp.swapaxes(codebooks, 1, 2).reshape(-1, codebooks.shape[1])
    def half(which, features, limit):
        chosen = jnp.concatenate([where, which[None].astype(jnp.int32)])
        return covariance_part(chosen, features, codes, table, limit)

    give, keep = half(1 - xl, features, FETCH_BYTES)
    theirs, features = lax.optimization_barrier((keep + swap(give, "core"), features))
    theirs = swap(theirs, "xl")
    give, keep = half(xl, features, VMEM_BYTES)
    middle = give.shape[0] // 2
    from_core = [swap(piece, "core") for piece in (give[:middle], give[middle:])]
    ours = lax.optimization_barrier(keep + jnp.concatenate(from_core, axis=0))
    current = ours + theirs
    dimensions = features.shape[1] * 16
    moves = (("z", 1), ("z", -1), ("y", 1), ("z", 2), ("y", 2))

    for sweep in range(ITERS):
        near = [send(current, axis, -d) for axis, d in moves]
        give, keep, *pair = gram_part(where, current, near[::-1])
        mine = sum_over_x(give, keep)
        ours = [mine] + [send(mine, "x", -d) for d in STEPS[1:]]
        if sweep == 0:
            squares = mine[:8, -128:]
            for bit in (1, 2):
                squares = squares + lax.ppermute(squares, "y", [(i, i ^ bit) for i in range(4)])
            ours[1], squares = lax.optimization_barrier((ours[1], squares))
            factor = start_scale * jnp.sqrt(dimensions / (jnp.sum(squares) + epsilon))
        else:
            factor = jnp.float32(1)
        shares = ours + [swap(piece, "core") for piece in ours]
        pieces, value = product_part(where, factor[None], shares, pair)
        received = [send(piece, axis, d) for piece, (axis, d) in zip(pieces, moves)]
        value = value + received[0] + received[1] + received[2]
        value, *received = lax.optimization_barrier((value, received[3], received[4]))
        if sweep < ITERS - 1:
            current = factor * (1.5 * current - 0.5 * (value + received[0] + received[1]))

    rows, width = current.shape
    piece = jax.ShapeDtypeStruct((rows // 4, width), F32)
    pieces = list(call(update_kernel, [piece] * 4, [where, current, value, *received]))
    for number, partner in enumerate(PARTNERS):
        if partner:
            pairs = [(i, i ^ partner) for i in range(4)]
            pieces[number] = lax.ppermute(pieces[number], ("xl", "core"), pairs)
    whole = jax.ShapeDtypeStruct((rows // 4, 4 * width), F32)
    return call(join_kernel, [whole], [where, *pieces])[0]


def solution(mesh):
    devices = mesh.devices.reshape(2, 2, 4, 4, 2)
    return jax.shard_map(
        on_device,
        mesh=Mesh(devices, AXES),
        in_specs=(
            P(("xl", "core"), ("z", "y")),
            P(("xl", "core"), "xh"),
            P("xh", None, None),
        ),
        out_specs=P(("z", "y", "xl", "core"), "xh"),
        check_vma=False,
    )
```
